128 devices in a mesh: peer: 32 (over x, y_hi, z), chan: 4 (over y_lo, core).
Axes of the slice: x: 4, y: 4 (y_hi: 2, y_lo: 2; y = y_hi * 2 + y_lo), z: 4, core: 2. Of those that a mesh axis runs over, the one named last changes fastest.
Arguments:
- images: bfloat16 [2, 64, 14, 14, 512], P(None, 'peer', None, None, 'chan'), may hold values from -12 to 12
- cotangent: bfloat16 [2, 32, 4, 14, 14, 512], P(None, 'peer', None, None, None, 'chan'), may hold values from -6 to 6
- image_ids: int32 [2, 32, 4], P(None, 'peer'), may hold values from 0 to 63, as said below
- counts: int32 [2, 32], P(None, 'peer'), may hold values from 1 to 4, 64 in all within a row
- hop_exponents: int32 [2], replicated, may hold values from 0 to 2
- param_mats: float32 [32, 2, 512, 2048], P('peer', None, None, 'chan'), may hold values from -0.25 to 0.25
- param_chans: float32 [32, 54, 512], P('peer', None, 'chan'), may hold values from -3 to 3
- param_bias: float32 [32, 2048], P('peer', 'chan'), may hold values from -3 to 3
- track_mats: float32 [32, 2, 512, 2048], P('peer', None, None, 'chan'), may hold values from -6 to 6
- track_chans: float32 [32, 54, 512], P('peer', None, 'chan'), may hold values from -6 to 6
- track_bias: float32 [32, 2048], P('peer', 'chan'), may hold values from -6 to 6
- grad_mats: float32 [32, 2, 512, 2048], P('peer', None, None, 'chan'), may hold values from -6 to 6
- grad_chans: float32 [32, 54, 512], P('peer', None, 'chan'), may hold values from -6 to 6
- grad_bias: float32 [32, 2048], P('peer', 'chan'), may hold values from -6 to 6
Outputs:
- new_param_mats: float32 [32, 2, 512, 2048], P('peer', None, None, 'chan')
- new_param_chans: float32 [32, 54, 512], P('peer', None, 'chan')
- new_param_bias: float32 [32, 2048], P('peer', 'chan')
- new_track_mats: float32 [32, 2, 512, 2048], P('peer', None, None, 'chan')
- new_track_chans: float32 [32, 54, 512], P('peer', None, 'chan')
- new_track_bias: float32 [32, 2048], P('peer', 'chan')
The draws below stay inside these ranges and needn't reach their ends.
Inputs may be any that keep to these rules, and one draw needn't show every extreme that they name: `image_ids`: entry s of a worker's list is read only where s is below its count; in each worker's list at most 2 entries name rows of one loader shard (rows b * 2 to (b + 1) * 2 - 1), and in every iteration some list has exactly 2 such entries. `counts`: in every iteration some worker has all 4 entries live.
All inputs are finite; a program needn't handle non-finite values. No bound on the sum of `counts` on one device may be relied on, other than what follows from the above.
Results may differ from the reference program's by a relative error of at most 0.006.
Values may be sent and summed in bfloat16 or wider, within the bound.
A program may use at most 128 MiB of HBM per device.

```python
import math
import jax
import jax.numpy as jnp
import numpy as np
from jax import lax

C = 512
FF = 2048
KS = 7
HGT = 14
WID = 14
ITERS = 2
PAIR_MAX = 2
B_LD = 2
L_MAX = 4
IMAGES = 64
N_PEER = 32


def draw_images(key, part):
    value_key, token_key = jax.random.split(jax.random.fold_in(key, 11))
    chan_pos = jnp.arange(C, dtype=jnp.float32) / (C - 1)
    token_draw = jax.random.uniform(token_key, (ITERS, IMAGES, HGT, WID, 1), jnp.float32)
    base = jax.random.normal(value_key, (ITERS, IMAGES, HGT, WID, C), jnp.float32)
    chan_scale = 0.6 * jnp.exp(1.0986123 * chan_pos)
    token_scale = 0.4 * jnp.exp(1.6094379 * token_draw)
    return jnp.clip(base * chan_scale * token_scale, -12.0, 12.0).astype(jnp.bfloat16)


def draw_image_ids(key, part):
    perm_key, offset_key = jax.random.split(jax.random.fold_in(key, 23))
    choices_all = jnp.broadcast_to(jnp.arange(PAIR_MAX * N_PEER, dtype=jnp.int32), (ITERS, N_PEER, PAIR_MAX * N_PEER))
    shuffled = jax.random.permutation(perm_key, choices_all, axis=-1, independent=True)
    loaders = shuffled[:, :, :L_MAX] // PAIR_MAX
    forced = jnp.zeros((ITERS, PAIR_MAX), jnp.int32)
    loaders = loaders.at[:, 0, :PAIR_MAX].set(forced)
    offsets = jax.random.randint(offset_key, (ITERS, N_PEER, L_MAX), 0, B_LD, jnp.int32)
    return loaders * B_LD + offsets


def shard_levels(stream_key, extent, cuts, smallest, largest):
    loudness = 1.0
    for dim, shards_of in cuts:
        steps = jax.random.uniform(jax.random.fold_in(jax.random.fold_in(stream_key, 6), dim), (shards_of,), jnp.float32, smallest / len(cuts), largest / len(cuts))
        loudness = loudness * jnp.repeat(jnp.exp(steps), extent[dim] // shards_of).reshape((-1,) + (1,) * (len(extent) - 1 - dim))
    return loudness


def length_profile(count, total, most, skew):
    portions = [(1 << 20) // math.isqrt(standing ** skew) + 1 for standing in range(2, count + 1)]
    spare, given = total - most - (count - 1), [1] * (count - 1)
    while spare > 0:
        movable = [i for i in range(count - 1) if given[i] < most]
        whole, left = sum([portions[i] for i in movable]), spare
        for i in movable:
            extra = min(most - given[i], max(1, left * portions[i] // whole), spare)
            given[i] = given[i] + extra
            spare = spare - extra
    return np.array([most] + given)


def ragged_sizes(own_key, count, total, bound, skew):
    if count == 2:
        one = jax.random.randint(own_key, (), max(1, total - bound), min(bound, total - 1) + 1)
        return jnp.stack([one, total - one])
    lengths = jnp.asarray(length_profile(count, total, bound, skew), jnp.int32)
    pairs = (count - 1) // 2
    source_of, taker = lengths[1:1 + 2 * pairs:2], lengths[2:2 + 2 * pairs:2]
    margin = jnp.minimum(source_of - 1, bound - taker)
    passed = jax.random.randint(jax.random.fold_in(own_key, 1), (pairs,), 0, 1 << 20) % (margin + 1)
    lengths = lengths.at[1:1 + 2 * pairs:2].set(source_of - passed).at[2:2 + 2 * pairs:2].set(taker + passed)
    return lengths[jax.random.permutation(jax.random.fold_in(own_key, 2), count)]


def noise(stream_key, dims, width, most, cuts=(), held_as=jnp.bfloat16):
    values = jax.random.normal(stream_key, dims, jnp.float32) * width
    if len(cuts) > 0:
        values = shard_levels(stream_key, dims, cuts, -0.22, 0.18) * values
    return jnp.clip(values, min=-most, max=most).astype(held_as)


def setup_inputs(seed: int = 0) -> dict:
    seeds = jax.random.split(jax.random.key(seed), 15)
    images = draw_images(jax.random.fold_in(seeds[14], 71), 0)
    cotangent = noise(seeds[1], (ITERS, N_PEER, L_MAX, HGT, WID, C), 1.0, 6.0, ((1, 32), (5, 4)))
    image_ids = draw_image_ids(jax.random.fold_in(seeds[14], 71), 0)
    counts = jax.vmap(lambda own: ragged_sizes(own, N_PEER, B_LD * N_PEER, L_MAX, 2))(jax.random.split(seeds[3], ITERS)).reshape((ITERS, N_PEER)).astype(jnp.int32)
    hop_exponents = jax.random.randint(seeds[4], (ITERS,), 0, 3).astype(jnp.int32)
    param_mats = noise(seeds[5], (N_PEER, 2, C, FF), C ** -0.5, 0.25, ((0, 32), (3, 4)), jnp.float32)
    param_chans = noise(seeds[6], (N_PEER, KS * KS + 5, C), 0.5, 3.0, ((0, 32), (2, 4)), jnp.float32)
    param_bias = noise(seeds[7], (N_PEER, FF), 0.5, 3.0, ((0, 32), (1, 4)), jnp.float32)
    track_mats = noise(seeds[8], (N_PEER, 2, C, FF), 1.0, 6.0, ((0, 32), (3, 4)), jnp.float32)
    track_chans = noise(seeds[9], (N_PEER, KS * KS + 5, C), 1.0, 6.0, ((0, 32), (2, 4)), jnp.float32)
    track_bias = noise(seeds[10], (N_PEER, FF), 1.0, 6.0, ((0, 32), (1, 4)), jnp.float32)
    grad_mats = noise(seeds[11], (N_PEER, 2, C, FF), 1.0, 6.0, ((0, 32), (3, 4)), jnp.float32)
    grad_chans = noise(seeds[12], (N_PEER, KS * KS + 5, C), 1.0, 6.0, ((0, 32), (2, 4)), jnp.float32)
    grad_bias = noise(seeds[13], (N_PEER, FF), 1.0, 6.0, ((0, 32), (1, 4)), jnp.float32)
    return dict(images=images, cotangent=cotangent, image_ids=image_ids, counts=counts, hop_exponents=hop_exponents, param_mats=param_mats, param_chans=param_chans, param_bias=param_bias, track_mats=track_mats, track_chans=track_chans, track_bias=track_bias, grad_mats=grad_mats, grad_chans=grad_chans, grad_bias=grad_bias)


EPS = 1e-06
LEARNING_RATE = 0.01
HIGHEST = lax.Precision.HIGHEST

def gelu_parts(hidden):
    normal_cdf = 0.5 * (1.0 + jax.scipy.special.erf(hidden * 0.7071067811865476))
    density = jnp.exp(-0.5 * hidden * hidden) * 0.3989422804014327
    return (hidden * normal_cdf, normal_cdf + hidden * density)

def padded_rows(source):
    half = KS // 2
    padded = jnp.pad(source, ((0, 0), (half, half), (half, half), (0, 0)))
    height, feature_width = (source.shape[1], source.shape[2])
    result = []
    for row_off in range(KS):
        result.append(jnp.stack([padded[:, row_off:row_off + height, col_off:col_off + feature_width, :] for col_off in range(KS)]))
    return result

def depthwise(source, kernel):
    total = jnp.zeros(source.shape, jnp.float32)
    for row_off, stacked in enumerate(padded_rows(source)):
        total = total + jnp.einsum('klhwc,kc->lhwc', stacked, kernel[row_off * KS:(row_off + 1) * KS], precision=HIGHEST)
    return total

def kernel_grad(source, grad_conv):
    pieces = []
    for stacked in padded_rows(source):
        pieces.append(jnp.einsum('klhwc,lhwc->kc', stacked, grad_conv, precision=HIGHEST))
    return jnp.concatenate(pieces, 0)

def worker_grad(matrices, channel_row_block, hidden_bias, picked, cot_slots, slot_count):
    filter_weight = KS * KS
    slots = picked.shape[0]
    feature_width = picked.shape[-1]
    valid = jnp.arange(slots, dtype=jnp.int32) < slot_count
    slot_weight = valid.astype(jnp.float32) / slot_count.astype(jnp.float32)
    source = picked.astype(jnp.float32) * valid.astype(jnp.float32)[:, None, None, None]
    conv_out = (depthwise(source, channel_row_block[:filter_weight]) + channel_row_block[filter_weight]).reshape(-1, feature_width)
    average = lax.optimization_barrier(jnp.sum(conv_out, 1)) / feature_width
    mean_removed = conv_out - average[:, None]
    variance = lax.optimization_barrier(jnp.sum(mean_removed * mean_removed, 1)) / feature_width
    inverse_deviation = lax.rsqrt(variance + EPS)
    standardized_input = mean_removed * inverse_deviation[:, None]
    norm_scale = channel_row_block[filter_weight + 1]
    normalized_rows = (standardized_input * norm_scale + channel_row_block[filter_weight + 2]).astype(jnp.bfloat16)
    w_first = matrices[0].astype(jnp.bfloat16)
    w_second = matrices[1].astype(jnp.bfloat16)
    hidden = jnp.dot(normalized_rows, w_first, preferred_element_type=jnp.float32) + hidden_bias
    act_full, slope = gelu_parts(hidden)
    activated = act_full.astype(jnp.bfloat16)
    branch = lax.dot_general(activated, w_second, (((1,), (1,)), ((), ())), preferred_element_type=jnp.float32) + channel_row_block[filter_weight + 3]
    weighted = (cot_slots.astype(jnp.float32) * slot_weight[:, None, None, None]).reshape(-1, feature_width)
    layer_scale = channel_row_block[filter_weight + 4]
    grad_scale = lax.optimization_barrier(jnp.sum(weighted * branch, 0))
    dbranch = layer_scale * weighted
    grad_bout = lax.optimization_barrier(jnp.sum(dbranch, 0))
    dbranch_low = dbranch.astype(jnp.bfloat16)
    grad_second = lax.dot_general(dbranch_low, activated, (((0,), (0,)), ((), ())), preferred_element_type=jnp.float32)
    dactivated = jnp.dot(dbranch_low, w_second, preferred_element_type=jnp.float32)
    dhidden = dactivated * slope
    grad_bin = lax.optimization_barrier(jnp.sum(dhidden, 0))
    dhidden_low = dhidden.astype(jnp.bfloat16)
    grad_first = lax.dot_general(normalized_rows, dhidden_low, (((0,), (0,)), ((), ())), preferred_element_type=jnp.float32)
    normalized_gradient = lax.dot_general(dhidden_low, w_first, (((1,), (1,)), ((), ())), preferred_element_type=jnp.float32)
    norm_scale_gradient = lax.optimization_barrier(jnp.sum(normalized_gradient * standardized_input, 0))
    grad_beta = lax.optimization_barrier(jnp.sum(normalized_gradient, 0))
    standardized_gradient = normalized_gradient * norm_scale
    first_moment = lax.optimization_barrier(jnp.sum(standardized_gradient, 1)) / feature_width
    second_moment = lax.optimization_barrier(jnp.sum(standardized_gradient * standardized_input, 1)) / feature_width
    convolution_gradient = (standardized_gradient - first_moment[:, None] - standardized_input * second_moment[:, None]) * inverse_deviation[:, None]
    grad_dbias = lax.optimization_barrier(jnp.sum(convolution_gradient, 0))
    grad_taps = kernel_grad(source, convolution_gradient.reshape(picked.shape))
    grad_rows = jnp.concatenate([grad_taps, grad_dbias[None], norm_scale_gradient[None], grad_beta[None], grad_bout[None], grad_scale[None]], 0)
    return (jnp.stack([grad_first, grad_second]), grad_rows, grad_bin)

def reference(images, cotangent, image_ids, counts, hop_exponents, param_mats, param_chans, param_bias, track_mats, track_chans, track_bias, grad_mats, grad_chans, grad_bias):
    params = (param_mats, param_chans, param_bias)
    tracker = (track_mats, track_chans, track_bias)
    previous = (grad_mats, grad_chans, grad_bias)
    workers = jnp.arange(N_PEER, dtype=jnp.int32)
    for iteration in range(ITERS):
        partner = jnp.bitwise_xor(workers, jnp.left_shift(jnp.int32(1), hop_exponents[iteration]))
        params = tuple((0.5 * (held + held[partner]) - LEARNING_RATE * track for held, track in zip(params, tracker)))
        images_now = images[iteration]

        def one_worker(packed):
            matrices, channel_row_block, hidden_bias, cot_slots, slot_ids, slot_count = packed
            picked = images_now[slot_ids]
            return worker_grad(matrices, channel_row_block, hidden_bias, picked, cot_slots, slot_count)
        fresh = lax.map(one_worker, (params[0], params[1], params[2], cotangent[iteration], image_ids[iteration], counts[iteration]))
        tracker = tuple((0.5 * (track + track[partner]) + new_grad - old_grad for track, new_grad, old_grad in zip(tracker, fresh, previous)))
        previous = fresh
    return (params[0], params[1], params[2], tracker[0], tracker[1], tracker[2])
```

```python
import functools

import jax
import jax.numpy as jnp
from jax import lax
from jax.experimental import pallas as pl
from jax.experimental.pallas import tpu as pltpu
from jax.sharding import PartitionSpec as P

KS = 7
TAPS = KS * KS
ITERS = 2
EPS = 1e-06
LEARNING_RATE = 0.01
MESH = pl.DeviceIdType.MESH
F32 = jnp.float32
BF16 = jnp.bfloat16
HIGHEST = lax.Precision.HIGHEST

SIDE = 14
PADW = 16
SLOTS = 4
SROWS = SIDE * PADW
ROWS = SLOTS * SROWS
CW = 128
C = 512
HID = 512
NCHUNK = 8
CROWS = 128
NCHAN = 4
STATW = ROWS + CW


def aligned(value, step):
    return pl.multiple_of(value, step)


def dot(a, b, ca, cb, precision=None):
    return lax.dot_general(
        a, b, (((ca,), (cb,)), ((), ())), precision=precision, preferred_element_type=F32
    )


def lane_sums(values):
    return dot(jnp.ones((8, CW), F32), values, 1, 1, HIGHEST)


def two_rows(first, second):
    row = lax.broadcasted_iota(jnp.int32, (8, first.shape[-1]), 0)
    return jnp.where(row == 0, first, jnp.where(row == 1, second, 0.0))


def two_columns(rows):
    row = lax.broadcasted_iota(jnp.int32, (8, 2 * CW), 0)
    lane = lax.broadcasted_iota(jnp.int32, (8, 2 * CW), 1)
    pick = jnp.where((lane < CW) & (row == 0), 1.0, 0.0) + jnp.where(
        (lane >= CW) & (row == 1), 1.0, 0.0
    )
    both = dot(rows, pick, 0, 0, HIGHEST)
    return both[:, :CW], both[:, CW:]


def kernel(t, hop, names, *refs):
    r = dict(zip(names, refs))
    first = t == 0
    peer = lax.axis_index("peer")
    chan = lax.axis_index("chan")
    my_z, my_y, my_x = peer % 4, (peer // 4) % 2, peer // 8
    core, side = chan % 2, chan // 2

    def at(new_peer, new_chan):
        return (new_peer, new_chan)

    c_core = side * 2 + 1 - core
    c_side = (1 - side) * 2 + core
    c_diag = (1 - side) * 2 + 1 - core
    d_core, d_side, d_diag = at(peer, c_core), at(peer, c_side), at(peer, c_diag)
    bit = (peer // (2**hop)) % 2
    d_hop = at(peer + (1 - 2 * bit) * (2**hop), chan)
    d_yhi = at(peer + (1 - 2 * my_y) * 4, chan)
    zs = [(my_z + d) % 4 for d in (1, 2, 3)]
    xs = [(my_x + d) % 4 for d in (1, 2, 3)]
    d_zs = [at(peer - my_z + z, chan) for z in zs]
    d_xs = [at(peer + (x - my_x) * 8, chan) for x in xs]

    counters = {"remote": 0, "local": 0}
    ends = []

    def take(kind, n):
        start = counters[kind]
        counters[kind] += n
        return start

    def remote(src, dst, device, index):
        return pltpu.make_async_remote_copy(
            src_ref=src,
            dst_ref=dst,
            send_sem=r["send"].at[index],
            recv_sem=r["recv"].at[index],
            device_id=device,
            device_id_type=MESH,
        )

    def push(src, dst, device):
        copy = remote(src, dst, device, take("remote", 1))
        copy.start()
        ends.append(copy.wait_send)
        return copy

    def local(src, dst):
        copy = pltpu.make_async_copy(src, dst, r["local"].at[take("local", 1)])
        copy.start()
        return copy

    P2, Y2, G2, F2 = r["P2"], r["Y2"], r["G2"], r["F2"]
    PB, PP, YB, YP, W = r["PB"], r["PP"], r["YB"], r["YP"], r["W"]

    def piece(ref, i):
        return ref.at[i // 4, pl.ds(aligned((i % 4) * CROWS, CROWS), CROWS), :]

    if first:
        G = [r["G0"], r["G1"]]
        own_rows = my_z * 4 + my_y * 2
        img_in = [local(r["images"].at[u], G[u].at[pl.ds(own_rows, 2)]) for u in range(2)]
    p_sem = take("local", NCHUNK)

    def p_load(i):
        return pltpu.make_async_copy(
            piece(r["pm"].at[0], i), piece(P2, i), r["local"].at[p_sem + i]
        )

    def start_p(i, carry):
        p_load(i).start()
        return carry

    lax.fori_loop(0, NCHUNK, start_p, 0)
    cot_in = local(r["cot"].at[t, 0], r["COTL"])
    y_in = local(r["ym"].at[0], Y2)
    g_in = local(r["gm"].at[0], G2)

    count = r["counts"][t, 0]

    def valid(s):
        return jnp.where(s < count, 1.0, 0.0).astype(F32)

    inv = 1.0 / jnp.full((1, CW), count.astype(F32))

    if first:
        IDV = r["IDV"]
        lane = lax.broadcasted_iota(jnp.int32, (8, 128), 1)
        row = lax.broadcasted_iota(jnp.int32, (8, 128), 0)
        tile = jnp.zeros((8, 128), jnp.int32)
        for u in range(2):
            for s in range(SLOTS):
                tile = jnp.where((row == u) & (lane == s), r["ids"][u, 0, s], tile)
        IDV[my_x] = tile

    barrier = pltpu.get_barrier_semaphore()
    greet = [d_core, d_side, d_diag] + ([d_yhi] + d_zs + d_xs if first else [d_hop])
    for device in greet:
        pl.semaphore_signal(barrier, inc=1, device_id=device, device_id_type=MESH)
    pl.semaphore_wait(barrier, len(greet))

    small = [
        push(r["pc"].at[0], r["RPC"], d_hop),
        push(r["pb"], r["RPB"], d_hop),
        push(r["yc"].at[0], r["RYC"], d_hop),
        push(r["yb"], r["RYB"], d_hop),
    ]

    fetch = {}
    if first:
        fetch["ids"] = [push(IDV.at[my_x], IDV.at[my_x], d) for d in d_xs]

    def images_begin(u):
        img_in[u].wait()
        mine = G[u].at[pl.ds(own_rows, 2)]
        fetch["y", u] = push(mine, mine, d_yhi)
        fetch["za", u] = [push(mine, mine, d) for d in d_zs]

    def images_second(u):
        fetch["y", u].wait_recv()
        other = G[u].at[pl.ds(my_z * 4 + (1 - my_y) * 2, 2)]
        fetch["zb", u] = [push(other, other, d) for d in d_zs]

    def wanted_row(source, u, s):
        ident = r["IDS"][source, u, s]
        return ((ident // 2) % 4) * 4 + ((ident // 8) % 2) * 2 + ident % 2

    def images_third(u):
        for copy in fetch["za", u] + fetch["zb", u]:
            copy.wait_recv()
        XS, XR = r["XS"], r["XR%d" % u]
        for j in range(3):
            for s in range(SLOTS):
                XS[u, j, s] = G[u][wanted_row(xs[j], u, s)]
        fetch["x", u] = [push(XS.at[u, j], XR.at[my_x], d_xs[j]) for j in range(3)]
        for s in range(SLOTS):
            XR[my_x, s] = G[u][wanted_row(my_x, u, s)]

    def images_end(u):
        for copy in fetch["x", u]:
            copy.wait_recv()

    def picked(u, s):
        return r["XR%d" % u][(r["IDS"][my_x, u, s] // 16) % 4, s]

    if first:
        images_begin(0)

    p_send = take("remote", NCHUNK)

    def p_copy(i):
        return remote(piece(PB, i), piece(PP, i), d_hop, p_send + i)

    def rows_of(i):
        return (i // 4, pl.ds(aligned((i % 4) * CROWS, CROWS), CROWS), slice(None))

    def send_p(i, carry):
        p_load(i).wait()
        PB[rows_of(i)] = P2[rows_of(i)].astype(BF16)
        p_copy(i).start()
        return carry

    lax.fori_loop(0, NCHUNK, send_p, 0)

    CF, CP = r["CF"], r["CP"]
    my_lanes = pl.ds(aligned(chan * CW, CW), CW)
    side_lanes = pl.ds(aligned(c_side * CW, CW), CW)
    CP[...] = jnp.zeros_like(CP)
    r["XP"][...] = jnp.zeros_like(r["XP"])
    cot_in.wait()
    cot_sum = jnp.zeros((1, CW), F32)
    for s in range(SLOTS):
        CP[s, :, 0:SIDE, :] = r["COTL"][s].astype(F32) * valid(s)
        flat = CP[s].reshape(SROWS, CW)
        cot_sum = cot_sum + jnp.sum(flat, 0, keepdims=True)
        CF[s * SROWS : (s + 1) * SROWS, my_lanes] = flat.astype(BF16)
    cot_core = push(CF.at[:, my_lanes], CF.at[:, my_lanes], d_core)
    cot_side = push(CF.at[:, my_lanes], CF.at[:, my_lanes], d_side)

    for copy in small:
        copy.wait_recv()
    qc, qb = r["qc"], r["qb"]
    qc[0] = 0.5 * (r["pc"][0] + r["RPC"][...]) - LEARNING_RATE * r["yc"][0]
    qb[...] = 0.5 * (r["pb"][...] + r["RPB"][...]) - LEARNING_RATE * r["yb"][...]

    def chan_row(k):
        return qc[0, k : k + 1, :]

    if first:
        images_second(0)
        for copy in fetch["ids"]:
            copy.wait_recv()
        ids_in = local(IDV, r["IDS"])
        ids_in.wait()
        images_third(0)
        images_begin(1)
        images_end(0)

    XP, SH, X = r["XP"], r["SH"], r["X"]
    for s in range(SLOTS):
        image = picked(0, s) if first else r["picked"][s]
        XP[s, 3 : 3 + SIDE, 3 : 3 + SIDE, :] = image.astype(F32) * valid(s)

    def shift(s, carry):
        for v in range(KS):
            SH[v, s] = XP[s, :, v : v + PADW, :]
        return carry

    lax.fori_loop(0, SLOTS, shift, 0)

    def conv_slot(s, carry):
        def column(v, acc):
            for u in range(KS):
                acc = acc + SH[v, s, u : u + SIDE] * qc[0, pl.ds(u * KS + v, 1), :]
            return acc

        acc = lax.fori_loop(0, KS, column, jnp.zeros((SIDE, PADW, CW), F32))
        X[pl.ds(aligned(s * SROWS, SROWS), SROWS), :] = acc.reshape(SROWS, CW) + chan_row(TAPS)
        return carry

    lax.fori_loop(0, SLOTS, conv_slot, 0)

    STR = r["STR"]
    conv_out = X[...]
    mean_here = jnp.sum(conv_out, 1, keepdims=True) * (1.0 / CW)
    centred = conv_out - mean_here
    mean_row = dot(jnp.full((8, CW), 1.0 / CW, F32), conv_out, 1, 1, HIGHEST)
    STR[chan, :, 0:ROWS] = two_rows(mean_row, lane_sums(centred * centred))
    STR[chan, :, ROWS:STATW] = jnp.broadcast_to(chan_row(TAPS + 4), (8, CW))
    stats = [push(STR.at[chan], STR.at[chan], d) for d in (d_core, d_side, d_diag)]
    cot_side.wait_recv()
    cot_far = push(CF.at[:, side_lanes], CF.at[:, side_lanes], d_core)
    for copy in stats:
        copy.wait_recv()
    means = [STR[j, 0:1, 0:ROWS] for j in range(NCHAN)]
    mean = (means[0] + means[1] + means[2] + means[3]) * 0.25
    squares = STR[0, 1:2, 0:ROWS] + STR[1, 1:2, 0:ROWS] + STR[2, 1:2, 0:ROWS] + STR[3, 1:2, 0:ROWS]
    for j in range(NCHAN):
        squares = squares + CW * (means[j] - mean) * (means[j] - mean)
    deviation = lax.rsqrt(squares * (1.0 / C) + EPS)
    mean_col, inv_col = two_columns(two_rows(mean, deviation))
    r["INV"][...] = inv_col
    xhat = (X[...] - mean_col) * inv_col
    X[...] = xhat
    NF = r["NF"]
    NF[:, my_lanes] = (xhat * chan_row(TAPS + 1) + chan_row(TAPS + 2)).astype(BF16)

    na, nb, nc = take("remote", SLOTS), take("remote", SLOTS), take("remote", SLOTS)

    def slot_rows(s):
        return pl.ds(aligned(s * SROWS, SROWS), SROWS)

    def norm_core(s):
        part = NF.at[slot_rows(s), my_lanes]
        return remote(part, part, d_core, na + s)

    def norm_side(s):
        part = NF.at[slot_rows(s), my_lanes]
        return remote(part, part, d_side, nb + s)

    def norm_far(s):
        part = NF.at[slot_rows(s), side_lanes]
        return remote(part, part, d_core, nc + s)

    def norm_send(s, carry):
        norm_side(s).start()
        norm_core(s).start()
        return carry

    lax.fori_loop(0, SLOTS, norm_send, 0)

    cot_core.wait_recv()
    cot_far.wait_recv()
    DB = r["DB"]
    for j in range(NCHAN):
        lanes = slice(j * CW, (j + 1) * CW)
        factor = inv * STR[j, 0:1, ROWS:STATW]
        DB[:, lanes] = (CF[:, lanes].astype(F32) * factor).astype(BF16)

    y_in.wait()

    def mix(i, carry):
        p_copy(i).wait_recv()
        q = 0.5 * (P2[rows_of(i)] + PP[rows_of(i)].astype(F32)) - LEARNING_RATE * Y2[rows_of(i)]
        P2[rows_of(i)] = q
        W[rows_of(i)] = q.astype(BF16)
        return carry

    lax.fori_loop(0, NCHUNK, mix, 0)
    q_out = local(P2, r["qm"].at[0])

    y_send = take("remote", NCHUNK)

    def y_copy(i):
        return remote(piece(YB, i), piece(YP, i), d_hop, y_send + i)

    def send_y(i, carry):
        YB[rows_of(i)] = Y2[rows_of(i)].astype(BF16)
        y_copy(i).start()
        return carry

    lax.fori_loop(0, NCHUNK, send_y, 0)

    ACT, DH, DP, R1, S2, R2, DN = (r[n] for n in ("ACT", "DH", "DP", "R1", "S2", "R2", "DN"))
    r1, r2 = take("remote", 2 * SLOTS), take("remote", SLOTS)

    def near_copy(s, b):
        lanes = pl.ds(aligned((b * 2 + 1 - core) * CW, CW), CW)
        return remote(DP.at[slot_rows(s), lanes], R1.at[b, slot_rows(s)], d_core, r1 + 2 * s + b)

    def far_copy(s):
        return remote(S2.at[slot_rows(s)], R2.at[slot_rows(s)], d_side, r2 + s)

    GB = r["GB"]
    GB[...] = jnp.zeros_like(GB)

    def slot_step(step, carry):
        @pl.when(step < SLOTS)
        def _():
            norm_side(step).wait_recv()
            norm_far(step).start()

        @pl.when((step > 0) & (step <= SLOTS))
        def _():
            s = step - 1
            norm_core(s).wait_recv()
            norm_far(s).wait_recv()
            rows = slot_rows(s)
            hidden = dot(NF[rows, :], W[0], 1, 0) + qb[...]
            cdf = 0.5 * (1.0 + lax.erf(hidden * 0.7071067811865476))
            density = jnp.exp(-0.5 * hidden * hidden) * 0.3989422804014327
            ACT[rows, :] = (hidden * cdf).astype(BF16)
            slope = cdf + hidden * density
            dhidden = dot(DB[rows, :], W[1], 1, 0) * slope
            GB[...] += jnp.sum(dhidden, 0, keepdims=True)
            low = dhidden.astype(BF16)
            DH[rows, :] = low
            DP[rows, :] = dot(low, W[0], 1, 1)
            near_copy(s, 0).start()
            near_copy(s, 1).start()

        @pl.when(step > 1)
        def _():
            s = step - 2
            rows = slot_rows(s)
            near_copy(s, 0).wait_recv()
            near_copy(s, 1).wait_recv()
            S2[rows, :] = (DP[rows, side_lanes] + R1[1 - side, rows, :]).astype(BF16)
            far_copy(s).start()
            DN[rows, :] = DP[rows, my_lanes] + R1[side, rows, :]

        return carry

    lax.fori_loop(0, SLOTS + 2, slot_step, 0)

    if first:
        images_second(1)

    BS, BR, GS = r["BS"], r["BR"], r["GS"]

    def scale_part(j, carry):
        lanes = pl.ds(aligned(j * CW, CW), CW)
        rows = pl.ds(aligned(j * CW, CW), CW)
        pair = dot(CF[:, lanes], ACT[...], 0, 0)
        weight = W[1, rows, :].astype(F32)
        GS[j] = dot(jnp.ones((8, HID), F32), pair * weight, 1, 1, HIGHEST)
        return carry

    lax.fori_loop(0, NCHAN, scale_part, 0)

    def far_wait(s, carry):
        far_copy(s).wait_recv()
        return carry

    lax.fori_loop(0, SLOTS, far_wait, 0)
    dnormed = DN[...] + R2[...].astype(F32)
    DN[...] = dnormed
    xhat = X[...]
    dxhat = dnormed * chan_row(TAPS + 1)
    sums = two_rows(lane_sums(dxhat), lane_sums(dxhat * xhat))
    for j in range(NCHAN):
        BS[j, :, 0:ROWS] = sums
        BS[j, :, ROWS:STATW] = GS[j]
    BR[chan] = BS[chan]
    back = [
        push(BS.at[c], BR.at[chan], d)
        for c, d in ((c_core, d_core), (c_side, d_side), (c_diag, d_diag))
    ]

    def mats_part(j, carry):
        lanes = pl.ds(aligned(j * CW, CW), CW)
        F2[0, lanes, :] = dot(NF[:, lanes], DH[...], 0, 0)
        F2[1, lanes, :] = dot(DB[:, lanes], ACT[...], 0, 0)
        return carry

    lax.fori_loop(0, NCHAN, mats_part, 0)
    if first:
        f_out = local(F2, r["fm"].at[0])

    if first:
        images_third(1)

    for copy in back:
        copy.wait_recv()
    totals = BR[0] + BR[1] + BR[2] + BR[3]
    mean_a, mean_b = two_columns(totals[:, 0:ROWS] * (1.0 / C))
    dnormed = DN[...]
    xhat = X[...]
    dconv = (dnormed * chan_row(TAPS + 1) - mean_a - xhat * mean_b) * r["INV"][...]
    DC, FC = r["DC"], r["FC"]
    DC[...] = dconv.reshape(SLOTS, SIDE, PADW, CW)
    FC[TAPS : TAPS + 1, :] = jnp.sum(dconv, 0, keepdims=True)
    FC[TAPS + 1 : TAPS + 2, :] = jnp.sum(dnormed * xhat, 0, keepdims=True)
    FC[TAPS + 2 : TAPS + 3, :] = jnp.sum(dnormed, 0, keepdims=True)
    FC[TAPS + 3 : TAPS + 4, :] = chan_row(TAPS + 4) * inv * cot_sum
    FC[TAPS + 4 : TAPS + 5, :] = inv * (totals[0:1, ROWS:STATW] + chan_row(TAPS + 3) * cot_sum)

    def tap_column(v, carry):
        def over(s, accs):
            grad = DC[s]
            return tuple(
                accs[u] + jnp.sum(SH[v, s, u : u + SIDE] * grad, 0) for u in range(KS)
            )

        accs = lax.fori_loop(0, SLOTS, over, tuple(jnp.zeros((PADW, CW), F32) for _ in range(KS)))
        for u in range(KS):
            FC[pl.ds(u * KS + v, 1), :] = jnp.sum(accs[u], 0, keepdims=True)
        return carry

    lax.fori_loop(0, KS, tap_column, 0)

    fresh = FC[0 : TAPS + 5, :]
    r["new_yc"][0] = 0.5 * (r["yc"][0] + r["RYC"][...]) + fresh - r["gc"][0]
    r["new_yb"][...] = 0.5 * (r["yb"][...] + r["RYB"][...]) + GB[...] - r["gb"][...]
    if first:
        r["fc"][0] = fresh
        r["fb"][...] = GB[...]
        images_end(1)
        for s in range(SLOTS):
            r["picked_next"][s] = picked(1, s)

    g_in.wait()
    out_sem = take("local", NCHUNK)

    def y_out(i):
        return pltpu.make_async_copy(
            piece(Y2, i), piece(r["new_ym"].at[0], i), r["local"].at[out_sem + i]
        )

    def track(i, carry):
        y_copy(i).wait_recv()
        at_i = rows_of(i)
        Y2[at_i] = 0.5 * (Y2[at_i] + YP[at_i].astype(F32)) + F2[at_i] - G2[at_i]
        y_out(i).start()
        return carry

    lax.fori_loop(0, NCHUNK, track, 0)

    def swaps_end(i, carry):
        p_copy(i).wait_send()
        y_copy(i).wait_send()
        y_out(i).wait()
        return carry

    lax.fori_loop(0, NCHUNK, swaps_end, 0)

    def slots_end(s, carry):
        norm_core(s).wait_send()
        norm_side(s).wait_send()
        norm_far(s).wait_send()
        near_copy(s, 0).wait_send()
        near_copy(s, 1).wait_send()
        far_copy(s).wait_send()
        return carry

    lax.fori_loop(0, SLOTS, slots_end, 0)
    for wait in ends:
        wait()
    q_out.wait()
    if first:
        f_out.wait()


def iteration(t, hop, state, images, cot, ids, counts):
    first = t == 0
    pm, pc, pb, ym, yc, yb, gm, gc, gb = state
    hbm = pl.BlockSpec(memory_space=pl.ANY)
    vmem = pl.BlockSpec(memory_space=pltpu.VMEM)
    smem = pl.BlockSpec(memory_space=pltpu.SMEM)
    ins = [("images", images, hbm), ("ids", ids, smem)] if first else [("picked", images, vmem)]
    ins += [("counts", counts, smem), ("cot", cot, hbm)]
    ins += [("pm", pm, hbm), ("pc", pc, vmem), ("pb", pb, vmem)]
    ins += [("ym", ym, hbm), ("yc", yc, vmem), ("yb", yb, vmem)]
    ins += [("gm", gm, hbm), ("gc", gc, vmem), ("gb", gb, vmem)]
    outs = [("qm", pm, hbm), ("qc", pc, vmem), ("qb", pb, vmem)]
    outs += [("new_ym", ym, hbm), ("new_yc", yc, vmem), ("new_yb", yb, vmem)]
    if first:
        outs += [("fm", gm, hbm), ("fc", gc, vmem), ("fb", gb, vmem)]
        outs += [("picked_next", jax.ShapeDtypeStruct((SLOTS, SIDE, SIDE, CW), BF16), vmem)]
    V = pltpu.VMEM
    mats = (2, C, HID)
    maps = (SIDE, SIDE, CW)
    scratch = {n: V(mats, F32) for n in ("P2", "Y2", "G2", "F2")}
    scratch |= {n: V(mats, BF16) for n in ("PB", "PP", "YB", "YP", "W")}
    scratch |= {n: V((ROWS, C), BF16) for n in ("NF", "CF", "DB", "ACT", "DH")}
    scratch |= {n: V((ROWS, CW), F32) for n in ("X", "INV", "DN")}
    scratch |= {n: V((ROWS, CW), BF16) for n in ("S2", "R2")}
    scratch |= {n: V((SLOTS, SIDE, PADW, CW), F32) for n in ("CP", "DC")}
    scratch |= {n: V((NCHAN, 8, STATW), F32) for n in ("STR", "BS", "BR")}
    scratch |= {n: V((TAPS + 5, CW), F32) for n in ("RPC", "RYC")}
    scratch |= {n: V((1, HID), F32) for n in ("RPB", "RYB", "GB")}
    scratch |= {
        "DP": V((ROWS, C), F32),
        "R1": V((2, ROWS, CW), F32),
        "GS": V((NCHAN, 8, CW), F32),
        "FC": V((TAPS + 7, CW), F32),
        "XP": V((SLOTS, SIDE + 6, 24, CW), F32),
        "SH": V((KS, SLOTS, SIDE + 6, PADW, CW), F32),
        "COTL": V((SLOTS,) + maps, BF16),
        "send": pltpu.SemaphoreType.DMA((96,)),
        "recv": pltpu.SemaphoreType.DMA((96,)),
        "local": pltpu.SemaphoreType.DMA((32,)),
    }
    if first:
        scratch |= {
            "G0": V((16,) + maps, BF16),
            "G1": V((16,) + maps, BF16),
            "XS": V((2, 3, SLOTS) + maps, BF16),
            "XR0": V((4, SLOTS) + maps, BF16),
            "XR1": V((4, SLOTS) + maps, BF16),
            "IDV": V((4, 8, 128), jnp.int32),
            "IDS": pltpu.SMEM((4, 8, 128), jnp.int32),
        }
    names = [n for n, _, _ in ins] + [n for n, _, _ in outs] + list(scratch)
    return pl.pallas_call(
        functools.partial(kernel, t, hop, names),
        out_shape=[jax.ShapeDtypeStruct(a.shape, a.dtype) for _, a, _ in outs],
        in_specs=[s for _, _, s in ins],
        out_specs=[s for _, _, s in outs],
        scratch_shapes=list(scratch.values()),
        compiler_params=pltpu.CompilerParams(
            collective_id=t * 3 + hop,
            has_side_effects=True,
            vmem_limit_bytes=58 * 1024 * 1024,
        ),
    )(*[a for _, a, _ in ins])


def on_device(images, cotangent, image_ids, counts, hop_exponents, *state):
    def branch(t, hop):
        def run(operands):
            source, state = operands
            return iteration(t, hop, state, source, cotangent, image_ids, counts)

        return run

    def step(t, source, state):
        return lax.switch(
            jnp.clip(hop_exponents[t], 0, 2), [branch(t, hop) for hop in range(3)], (source, state)
        )

    out = step(0, images, state)
    return tuple(step(1, out[9], tuple(out[:9])))


def solution(mesh):
    mats, chans, bias = P("peer", None, None, "chan"), P("peer", None, "chan"), P("peer", "chan")
    in_specs = (
        P(None, "peer", None, None, "chan"),
        P(None, "peer", None, None, None, "chan"),
        P(None, "peer", None),
        P(None, "peer"),
        P(),
    ) + (mats, chans, bias) * 3
    return jax.shard_map(
        on_device, mesh=mesh, in_specs=in_specs, out_specs=(mats, chans, bias) * 2, check_vma=False
    )
```

```python
import functools

import jax
import jax.numpy as jnp
from jax import lax
from jax.experimental import pallas as pl
from jax.experimental.pallas import tpu as pltpu
from jax.sharding import PartitionSpec as P

KS = 7
TAPS = KS * KS
ITERS = 2
EPS = 1e-06
LEARNING_RATE = 0.01
MESH = pl.DeviceIdType.MESH
F32 = jnp.float32
BF16 = jnp.bfloat16
HIGHEST = lax.Precision.HIGHEST

SIDE = 14
PADW = 16
HALF = SIDE // 2
SLOTS = 4
SROWS = SIDE * PADW
ROWS = SLOTS * SROWS
CW = 128
C = 512
HID = 512
NCHUNK = 8
CROWS = 128
NCHAN = 4
STATW = ROWS + CW


def aligned(value, step):
    return pl.multiple_of(value, step)


def dot(a, b, ca, cb, precision=None):
    return lax.dot_general(
        a, b, (((ca,), (cb,)), ((), ())), precision=precision, preferred_element_type=F32
    )


def lane_sums(values):
    return dot(jnp.ones((8, CW), F32), values, 1, 1, HIGHEST)


def two_rows(first, second):
    row = lax.broadcasted_iota(jnp.int32, (8, first.shape[-1]), 0)
    return jnp.where(row == 0, first, jnp.where(row == 1, second, 0.0))


def two_columns(rows):
    row = lax.broadcasted_iota(jnp.int32, (8, 2 * CW), 0)
    lane = lax.broadcasted_iota(jnp.int32, (8, 2 * CW), 1)
    pick = jnp.where((lane < CW) & (row == 0), 1.0, 0.0) + jnp.where(
        (lane >= CW) & (row == 1), 1.0, 0.0
    )
    both = dot(rows, pick, 0, 0, HIGHEST)
    return both[:, :CW], both[:, CW:]


def kernel(t, hop, names, *refs):
    r = dict(zip(names, refs))
    first = t == 0
    peer = lax.axis_index("peer")
    chan = lax.axis_index("chan")
    my_z, my_y, my_x = peer % 4, (peer // 4) % 2, peer // 8
    core, side = chan % 2, chan // 2

    def at(new_peer, new_chan):
        return (new_peer, new_chan)

    c_core = side * 2 + 1 - core
    c_side = (1 - side) * 2 + core
    c_diag = (1 - side) * 2 + 1 - core
    d_core, d_side, d_diag = at(peer, c_core), at(peer, c_side), at(peer, c_diag)
    bit = (peer // (2**hop)) % 2
    d_hop = at(peer + (1 - 2 * bit) * (2**hop), chan)
    d_yhi = at(peer + (1 - 2 * my_y) * 4, chan)
    zs = [(my_z + d) % 4 for d in (1, 2, 3)]
    xs = [(my_x + d) % 4 for d in (1, 2, 3)]
    d_zs = [at(peer - my_z + z, chan) for z in zs]
    d_xs = [at(peer + (x - my_x) * 8, chan) for x in xs]

    counters = {"remote": 0, "local": 0}
    ends = []

    def take(kind, n):
        start = counters[kind]
        counters[kind] += n
        return start

    def remote(src, dst, device, index):
        return pltpu.make_async_remote_copy(
            src_ref=src,
            dst_ref=dst,
            send_sem=r["send"].at[index],
            recv_sem=r["recv"].at[index],
            device_id=device,
            device_id_type=MESH,
        )

    def push(src, dst, device):
        copy = remote(src, dst, device, take("remote", 1))
        copy.start()
        ends.append(copy.wait_send)
        return copy

    def local(src, dst):
        copy = pltpu.make_async_copy(src, dst, r["local"].at[take("local", 1)])
        copy.start()
        return copy

    P2, Y2, G2, F2 = r["P2"], r["Y2"], r["G2"], r["F2"]
    PB, PP, YB, YP, W = r["PB"], r["PP"], r["YB"], r["YP"], r["W"]

    def piece(ref, i):
        return ref.at[i // 4, pl.ds(aligned((i % 4) * CROWS, CROWS), CROWS), :]

    if first:
        G = [[r["G%d%d" % (u, h)] for h in range(2)] for u in range(2)]
        z_step, y_step = (4, 2) if hop == 2 else (2, 8)

        def block(u, h, z, y):
            return G[u][h].at[pl.ds(z * z_step + y * y_step, 2)]

        img_in = {
            (u, h): local(
                r["images"].at[u, :, pl.ds(h * HALF, HALF)], block(u, h, my_z, my_y)
            )
            for u in range(2)
            for h in range(2)
        }
    p_sem = take("local", NCHUNK)

    def p_load(i):
        return pltpu.make_async_copy(
            piece(r["pm"].at[0], i), piece(P2, i), r["local"].at[p_sem + i]
        )

    def start_p(i, carry):
        p_load(i).start()
        return carry

    lax.fori_loop(0, NCHUNK, start_p, 0)
    CF = r["CF"]
    my_lanes = pl.ds(aligned(chan * CW, CW), CW)
    side_lanes = pl.ds(aligned(c_side * CW, CW), CW)
    cot_in = local(r["cot"].at[t], CF.at[:, my_lanes])
    y_in = local(r["ym"].at[0], Y2)
    g_in = local(r["gm"].at[0], G2)

    count = r["counts"][0, t]

    def valid(s):
        return jnp.where(s < count, 1.0, 0.0).astype(F32)

    inv = 1.0 / jnp.full((1, CW), count.astype(F32))

    if first:
        IDV = r["IDV"]
        lane = lax.broadcasted_iota(jnp.int32, (8, 128), 1)
        row = lax.broadcasted_iota(jnp.int32, (8, 128), 0)
        tile = jnp.zeros((8, 128), jnp.int32)
        for u in range(2):
            for s in range(SLOTS):
                tile = jnp.where((row == u) & (lane == s), r["ids"][u, 0, s], tile)
        IDV[my_x] = tile

    barrier = pltpu.get_barrier_semaphore()
    greet = [d_core, d_side, d_diag] + ([d_yhi] + d_zs + d_xs if first else [d_hop])
    for device in greet:
        pl.semaphore_signal(barrier, inc=1, device_id=device, device_id_type=MESH)
    pl.semaphore_wait(barrier, len(greet))

    small = [
        push(r["pc"], r["RPC"], d_hop),
        push(r["pb"], r["RPB"], d_hop),
        push(r["yc"], r["RYC"], d_hop),
        push(r["yb"], r["RYB"], d_hop),
    ]

    fetch = {}
    if first:
        fetch["ids"] = [push(IDV.at[my_x], IDV.at[my_x], d) for d in d_xs]

    if first:
        z_from = [(my_z - d) % 4 for d in (1, 2, 3)]
        y_part = ([d_yhi], [(my_z, 1 - my_y)])
        z_part = (d_zs, [(z, my_y) for z in z_from])
        (near_to, near_from), (next_to, next_from) = (
            (y_part, z_part) if hop == 2 else (z_part, y_part)
        )

    def images_begin(u):
        for h in range(2):
            img_in[u, h].wait()
            mine = block(u, h, my_z, my_y)
            fetch["near", u, h] = [push(mine, mine, d) for d in near_to]
            fetch["next", u, h] = [push(mine, mine, d) for d in next_to]

    def images_second(u):
        for h in range(2):
            for copy, place in zip(fetch["near", u, h], near_from):
                copy.wait_recv()
                part = block(u, h, *place)
                fetch["next", u, h] += [push(part, part, d) for d in next_to]

    def wanted_row(source, u, s):
        ident = r["IDS"][source, u, s]
        return ((ident // 2) % 4) * z_step + ((ident // 8) % 2) * y_step + ident % 2

    def images_third(u):
        for h in range(2):
            for copy in fetch["next", u, h]:
                copy.wait_recv()
            XS, XR = r["XS"], r["XR%d%d" % (u, h)]
            fetch["x", u, h] = []
            for j in range(3):
                for s in range(SLOTS):
                    XS[u, h, j, s] = G[u][h][wanted_row(xs[j], u, s)]
                fetch["x", u, h].append(push(XS.at[u, h, j], XR.at[my_x], d_xs[j]))
            for s in range(SLOTS):
                XR[my_x, s] = G[u][h][wanted_row(my_x, u, s)]

    def images_end(u):
        for h in range(2):
            for copy in fetch["x", u, h]:
                copy.wait_recv()

    def picked(u, h, s):
        return r["XR%d%d" % (u, h)][(r["IDS"][my_x, u, s] // 16) % 4, s]

    if first:
        images_begin(0)

    p_send = take("remote", NCHUNK)

    def p_copy(i):
        return remote(piece(PB, i), piece(PP, i), d_hop, p_send + i)

    def rows_of(i):
        return (i // 4, pl.ds(aligned((i % 4) * CROWS, CROWS), CROWS), slice(None))

    def send_p(i, carry):
        p_load(i).wait()
        PB[rows_of(i)] = P2[rows_of(i)].astype(BF16)
        p_copy(i).start()
        return carry

    lax.fori_loop(0, NCHUNK, send_p, 0)

    r["XP"][...] = jnp.zeros_like(r["XP"])
    cot_in.wait()
    cot_core = push(CF.at[:, my_lanes], CF.at[:, my_lanes], d_core)
    cot_side = push(CF.at[:, my_lanes], CF.at[:, my_lanes], d_side)

    for copy in small:
        copy.wait_recv()
    qc, qb = r["qc"], r["qb"]
    qc[...] = 0.5 * (r["pc"][...] + r["RPC"][...]) - LEARNING_RATE * r["yc"][...]
    qb[...] = 0.5 * (r["pb"][...] + r["RPB"][...]) - LEARNING_RATE * r["yb"][...]

    def chan_row(k):
        return qc[k]

    if first:
        images_second(0)
        for copy in fetch["ids"]:
            copy.wait_recv()
        ids_in = local(IDV, r["IDS"])
        ids_in.wait()
        images_third(0)
        images_begin(1)
        images_end(0)

    XP, SH, X = r["XP"], r["SH"], r["X"]
    for s in range(SLOTS):
        for h in range(2):
            image = picked(0, h, s) if first else r["picked"][s, h * HALF : (h + 1) * HALF]
            top = 3 + h * HALF
            XP[s, top : top + HALF, 3 : 3 + SIDE, :] = image.astype(F32) * valid(s)

    def shift(s, carry):
        for v in range(KS):
            SH[v, s] = XP[s, :, v : v + PADW, :]
        return carry

    lax.fori_loop(0, SLOTS, shift, 0)

    def conv_slot(s, carry):
        def column(v, acc):
            for u in range(KS):
                acc = acc + SH[v, s, u : u + SIDE] * qc[u * KS + v]
            return acc

        acc = lax.fori_loop(0, KS, column, jnp.zeros((SIDE, PADW, CW), F32))
        X[pl.ds(aligned(s * SROWS, SROWS), SROWS), :] = acc.reshape(SROWS, CW) + chan_row(TAPS)
        return carry

    lax.fori_loop(0, SLOTS, conv_slot, 0)

    STR = r["STR"]
    conv_out = X[...]
    mean_here = jnp.sum(conv_out, 1, keepdims=True) * (1.0 / CW)
    centred = conv_out - mean_here
    mean_row = dot(jnp.full((8, CW), 1.0 / CW, F32), conv_out, 1, 1, HIGHEST)
    STR[chan, :, 0:ROWS] = two_rows(mean_row, lane_sums(centred * centred))
    STR[chan, :, ROWS:STATW] = jnp.broadcast_to(chan_row(TAPS + 4), (8, CW))
    stats = [push(STR.at[chan], STR.at[chan], d) for d in (d_core, d_side, d_diag)]
    cot_side.wait_recv()
    cot_far = push(CF.at[:, side_lanes], CF.at[:, side_lanes], d_core)
    for copy in stats:
        copy.wait_recv()
    means = [STR[j, 0:1, 0:ROWS] for j in range(NCHAN)]
    mean = (means[0] + means[1] + means[2] + means[3]) * 0.25
    squares = STR[0, 1:2, 0:ROWS] + STR[1, 1:2, 0:ROWS] + STR[2, 1:2, 0:ROWS] + STR[3, 1:2, 0:ROWS]
    for j in range(NCHAN):
        squares = squares + CW * (means[j] - mean) * (means[j] - mean)
    deviation = lax.rsqrt(squares * (1.0 / C) + EPS)
    mean_col, inv_col = two_columns(two_rows(mean, deviation))
    r["INV"][...] = inv_col
    xhat = (X[...] - mean_col) * inv_col
    X[...] = xhat
    NF = r["NF"]
    NF[:, my_lanes] = (xhat * chan_row(TAPS + 1) + chan_row(TAPS + 2)).astype(BF16)

    na, nb, nc = take("remote", SLOTS), take("remote", SLOTS), take("remote", SLOTS)

    def slot_rows(s):
        return pl.ds(aligned(s * SROWS, SROWS), SROWS)

    def norm_core(s):
        part = NF.at[slot_rows(s), my_lanes]
        return remote(part, part, d_core, na + s)

    def norm_side(s):
        part = NF.at[slot_rows(s), my_lanes]
        return remote(part, part, d_side, nb + s)

    def norm_far(s):
        part = NF.at[slot_rows(s), side_lanes]
        return remote(part, part, d_core, nc + s)

    def norm_send(s, carry):
        norm_side(s).start()
        norm_core(s).start()
        return carry

    lax.fori_loop(0, SLOTS, norm_send, 0)

    if first:
        images_second(1)

    cot_core.wait_recv()
    cot_far.wait_recv()
    DB = r["DB"]
    cot_sum = jnp.sum(CF[:, my_lanes].astype(F32), 0, keepdims=True)
    for j in range(NCHAN):
        lanes = slice(j * CW, (j + 1) * CW)
        factor = inv * STR[j, 0:1, ROWS:STATW]
        DB[:, lanes] = (CF[:, lanes].astype(F32) * factor).astype(BF16)

    y_in.wait()

    def mix(i, carry):
        p_copy(i).wait_recv()
        q = 0.5 * (P2[rows_of(i)] + PP[rows_of(i)].astype(F32)) - LEARNING_RATE * Y2[rows_of(i)]
        P2[rows_of(i)] = q
        W[rows_of(i)] = q.astype(BF16)
        return carry

    lax.fori_loop(0, NCHUNK, mix, 0)
    q_out = local(P2, r["qm"].at[0])

    y_send = take("remote", NCHUNK)

    def y_copy(i):
        return remote(piece(YB, i), piece(YP, i), d_hop, y_send + i)

    def send_y(i, carry):
        YB[rows_of(i)] = Y2[rows_of(i)].astype(BF16)
        y_copy(i).start()
        return carry

    if hop != 2:
        lax.fori_loop(0, NCHUNK, send_y, 0)

    if first:
        images_third(1)

    ACT, DH, DP, R1, S2, R2, DN = (r[n] for n in ("ACT", "DH", "DP", "R1", "S2", "R2", "DN"))
    r1, r2 = take("remote", 2 * SLOTS), take("remote", SLOTS)

    def near_copy(s, b):
        lanes = pl.ds(aligned((b * 2 + 1 - core) * CW, CW), CW)
        return remote(DP.at[slot_rows(s), lanes], R1.at[b, slot_rows(s)], d_core, r1 + 2 * s + b)

    def far_copy(s):
        return remote(S2.at[slot_rows(s)], R2.at[slot_rows(s)], d_side, r2 + s)

    GB = r["GB"]
    GB[...] = jnp.zeros_like(GB)

    def slot_step(step, carry):
        if hop == 2:
            send_y(step, carry)

        @pl.when(step < SLOTS)
        def _():
            norm_side(step).wait_recv()
            norm_far(step).start()

        @pl.when((step > 0) & (step <= SLOTS))
        def _():
            s = step - 1
            norm_core(s).wait_recv()
            norm_far(s).wait_recv()
            rows = slot_rows(s)
            hidden = dot(NF[rows, :], W[0], 1, 0) + qb[...]
            cdf = 0.5 * (1.0 + lax.erf(hidden * 0.7071067811865476))
            density = jnp.exp(-0.5 * hidden * hidden) * 0.3989422804014327
            ACT[rows, :] = (hidden * cdf).astype(BF16)
            slope = cdf + hidden * density
            dhidden = dot(DB[rows, :], W[1], 1, 0) * slope
            GB[...] += jnp.sum(dhidden, 0, keepdims=True)
            low = dhidden.astype(BF16)
            DH[rows, :] = low
            DP[rows, :] = dot(low, W[0], 1, 1)
            near_copy(s, 0).start()
            near_copy(s, 1).start()

        @pl.when(step > 1)
        def _():
            s = step - 2
            rows = slot_rows(s)
            near_copy(s, 0).wait_recv()
            near_copy(s, 1).wait_recv()
            S2[rows, :] = (DP[rows, side_lanes] + R1[1 - side, rows, :]).astype(BF16)
            far_copy(s).start()
            DN[rows, :] = DP[rows, my_lanes] + R1[side, rows, :]

        return carry

    lax.fori_loop(0, SLOTS + 2, slot_step, 0)
    if hop == 2:
        lax.fori_loop(SLOTS + 2, NCHUNK, send_y, 0)

    BS, BR, GS = r["BS"], r["BR"], r["GS"]

    def scale_part(j, carry):
        lanes = pl.ds(aligned(j * CW, CW), CW)
        rows = pl.ds(aligned(j * CW, CW), CW)
        pair = dot(CF[:, lanes], ACT[...], 0, 0)
        weight = W[1, rows, :].astype(F32)
        GS[j] = dot(jnp.ones((8, HID), F32), pair * weight, 1, 1, HIGHEST)
        return carry

    lax.fori_loop(0, NCHAN, scale_part, 0)

    def far_wait(s, carry):
        far_copy(s).wait_recv()
        return carry

    lax.fori_loop(0, SLOTS, far_wait, 0)
    dnormed = DN[...] + R2[...].astype(F32)
    DN[...] = dnormed
    xhat = X[...]
    dxhat = dnormed * chan_row(TAPS + 1)
    sums = two_rows(lane_sums(dxhat), lane_sums(dxhat * xhat))
    for j in range(NCHAN):
        BS[j, :, 0:ROWS] = sums
        BS[j, :, ROWS:STATW] = GS[j]
    BR[chan] = BS[chan]
    back = [
        push(BS.at[c], BR.at[chan], d)
        for c, d in ((c_core, d_core), (c_side, d_side), (c_diag, d_diag))
    ]

    def mats_part(j, carry):
        lanes = pl.ds(aligned(j * CW, CW), CW)
        F2[0, lanes, :] = dot(NF[:, lanes], DH[...], 0, 0)
        F2[1, lanes, :] = dot(DB[:, lanes], ACT[...], 0, 0)
        return carry

    lax.fori_loop(0, NCHAN, mats_part, 0)
    if first:
        f_out = local(F2, r["fm"].at[0])

    for copy in back:
        copy.wait_recv()
    totals = BR[0] + BR[1] + BR[2] + BR[3]
    mean_a, mean_b = two_columns(totals[:, 0:ROWS] * (1.0 / C))
    dnormed = DN[...]
    xhat = X[...]
    dconv = (dnormed * chan_row(TAPS + 1) - mean_a - xhat * mean_b) * r["INV"][...]
    DC, FC = r["DC"], r["FC"]
    DC[...] = dconv.reshape(SLOTS, SIDE, PADW, CW)
    FC[TAPS] = jnp.sum(dconv, 0, keepdims=True)
    FC[TAPS + 1] = jnp.sum(dnormed * xhat, 0, keepdims=True)
    FC[TAPS + 2] = jnp.sum(dnormed, 0, keepdims=True)
    FC[TAPS + 3] = chan_row(TAPS + 4) * inv * cot_sum
    FC[TAPS + 4] = inv * (totals[0:1, ROWS:STATW] + chan_row(TAPS + 3) * cot_sum)

    def tap_column(v, carry):
        def over(s, accs):
            grad = DC[s]
            return tuple(
                accs[u] + jnp.sum(SH[v, s, u : u + SIDE] * grad, 0) for u in range(KS)
            )

        accs = lax.fori_loop(0, SLOTS, over, tuple(jnp.zeros((PADW, CW), F32) for _ in range(KS)))
        for u in range(KS):
            FC[u * KS + v] = jnp.sum(accs[u], 0, keepdims=True)
        return carry

    lax.fori_loop(0, KS, tap_column, 0)

    fresh = FC[...]
    r["new_yc"][...] = 0.5 * (r["yc"][...] + r["RYC"][...]) + fresh - r["gc"][...]
    r["new_yb"][...] = 0.5 * (r["yb"][...] + r["RYB"][...]) + GB[...] - r["gb"][...]
    if first:
        r["fc"][...] = fresh
        r["fb"][...] = GB[...]
        images_end(1)
        for s in range(SLOTS):
            for h in range(2):
                r["picked_next"][s, h * HALF : (h + 1) * HALF] = picked(1, h, s)

    g_in.wait()
    out_sem = take("local", NCHUNK)

    def y_out(i):
        return pltpu.make_async_copy(
            piece(Y2, i), piece(r["new_ym"].at[0], i), r["local"].at[out_sem + i]
        )

    def track(i, carry):
        y_copy(i).wait_recv()
        at_i = rows_of(i)
        Y2[at_i] = 0.5 * (Y2[at_i] + YP[at_i].astype(F32)) + F2[at_i] - G2[at_i]
        y_out(i).start()
        return carry

    lax.fori_loop(0, NCHUNK, track, 0)

    def swaps_end(i, carry):
        p_copy(i).wait_send()
        y_copy(i).wait_send()
        y_out(i).wait()
        return carry

    lax.fori_loop(0, NCHUNK, swaps_end, 0)

    def slots_end(s, carry):
        norm_core(s).wait_send()
        norm_side(s).wait_send()
        norm_far(s).wait_send()
        near_copy(s, 0).wait_send()
        near_copy(s, 1).wait_send()
        far_copy(s).wait_send()
        return carry

    lax.fori_loop(0, SLOTS, slots_end, 0)
    for wait in ends:
        wait()
    q_out.wait()
    if first:
        f_out.wait()


def iteration(t, hop, state, images, cot, ids, counts):
    first = t == 0
    pm, pc, pb, ym, yc, yb, gm, gc, gb = state
    hbm = pl.BlockSpec(memory_space=pl.ANY)
    vmem = pl.BlockSpec(memory_space=pltpu.VMEM)
    smem = pl.BlockSpec(memory_space=pltpu.SMEM)
    ins = [("images", images, hbm), ("ids", ids, smem)] if first else [("picked", images, vmem)]
    ins += [("counts", counts, smem), ("cot", cot, hbm)]
    ins += [("pm", pm, hbm), ("pc", pc, vmem), ("pb", pb, vmem)]
    ins += [("ym", ym, hbm), ("yc", yc, vmem), ("yb", yb, vmem)]
    ins += [("gm", gm, hbm), ("gc", gc, vmem), ("gb", gb, vmem)]
    outs = [("qm", pm, hbm), ("qc", pc, vmem), ("qb", pb, vmem)]
    outs += [("new_ym", ym, hbm), ("new_yc", yc, vmem), ("new_yb", yb, vmem)]
    if first:
        outs += [("fm", gm, hbm), ("fc", gc, vmem), ("fb", gb, vmem)]
        outs += [("picked_next", jax.ShapeDtypeStruct((SLOTS, SIDE, SIDE, CW), BF16), vmem)]
    V = pltpu.VMEM
    mats = (2, C, HID)
    half = (HALF, SIDE, CW)
    scratch = {n: V(mats, F32) for n in ("P2", "Y2", "G2", "F2")}
    scratch |= {n: V(mats, BF16) for n in ("PB", "PP", "YB", "YP", "W")}
    scratch |= {n: V((ROWS, C), BF16) for n in ("NF", "CF", "DB", "ACT", "DH")}
    scratch |= {n: V((ROWS, CW), F32) for n in ("X", "INV", "DN")}
    scratch |= {n: V((ROWS, CW), BF16) for n in ("S2", "R2")}
    scratch |= {n: V((SLOTS, SIDE, PADW, CW), F32) for n in ("DC",)}
    scratch |= {n: V((NCHAN, 8, STATW), F32) for n in ("STR", "BS", "BR")}
    scratch |= {n: V((TAPS + 5, 1, CW), F32) for n in ("RPC", "RYC", "FC")}
    scratch |= {n: V((1, HID), F32) for n in ("RPB", "RYB", "GB")}
    scratch |= {
        "DP": V((ROWS, C), F32),
        "R1": V((2, ROWS, CW), F32),
        "GS": V((NCHAN, 8, CW), F32),
        "XP": V((SLOTS, SIDE + 6, 24, CW), F32),
        "SH": V((KS, SLOTS, SIDE + 6, PADW, CW), F32),
        "send": pltpu.SemaphoreType.DMA((128,)),
        "recv": pltpu.SemaphoreType.DMA((128,)),
        "local": pltpu.SemaphoreType.DMA((32,)),
    }
    if first:
        for u in range(2):
            for h in range(2):
                scratch["G%d%d" % (u, h)] = V((16,) + half, BF16)
                scratch["XR%d%d" % (u, h)] = V((4, SLOTS) + half, BF16)
        scratch |= {
            "XS": V((2, 2, 3, SLOTS) + half, BF16),
            "IDV": V((4, 8, 128), jnp.int32),
            "IDS": pltpu.SMEM((4, 8, 128), jnp.int32),
        }
    names = [n for n, _, _ in ins] + [n for n, _, _ in outs] + list(scratch)
    return pl.pallas_call(
        functools.partial(kernel, t, hop, names),
        out_shape=[jax.ShapeDtypeStruct(a.shape, a.dtype) for _, a, _ in outs],
        in_specs=[s for _, _, s in ins],
        out_specs=[s for _, _, s in outs],
        scratch_shapes=list(scratch.values()),
        compiler_params=pltpu.CompilerParams(
            collective_id=t * 3 + hop,
            has_side_effects=True,
            vmem_limit_bytes=58 * 1024 * 1024,
        ),
    )(*[a for _, a, _ in ins])


def on_device(images, cotangent, image_ids, counts, hop_exponents, *state):
    live = jnp.arange(SLOTS, dtype=jnp.int32)[None, :] < counts
    masked = jnp.where(live[:, :, None, None, None], cotangent[:, 0], 0)
    cot = jnp.pad(masked, ((0, 0), (0, 0), (0, 0), (0, PADW - SIDE), (0, 0)))
    cot = cot.reshape(ITERS, ROWS, CW)
    counts = counts.T

    def turned(values):
        return tuple(a.transpose(1, 0, 2) if i % 3 == 1 else a for i, a in enumerate(values))

    def branch(t, hop):
        def run(operands):
            source, state = operands
            return iteration(t, hop, state, source, cot, image_ids, counts)

        return run

    def step(t, source, state):
        return lax.switch(
            jnp.clip(hop_exponents[t], 0, 2), [branch(t, hop) for hop in range(3)], (source, state)
        )

    out = step(0, images, turned(state))
    return turned(step(1, out[9], tuple(out[:9])))


def solution(mesh):
    mats, chans, bias = P("peer", None, None, "chan"), P("peer", None, "chan"), P("peer", "chan")
    in_specs = (
        P(None, "peer", None, None, "chan"),
        P(None, "peer", None, None, None, "chan"),
        P(None, "peer", None),
        P(None, "peer"),
        P(),
    ) + (mats, chans, bias) * 3
    return jax.shard_map(
        on_device, mesh=mesh, in_specs=in_specs, out_specs=(mats, chans, bias) * 2, check_vma=False
    )
```

```python
import functools

import jax
import jax.numpy as jnp
from jax import lax
from jax.experimental import pallas as pl
from jax.experimental.pallas import tpu as pltpu
from jax.sharding import PartitionSpec as P

KS = 7
TAPS = KS * KS
ITERS = 2
EPS = 1e-06
LEARNING_RATE = 0.01
MESH = pl.DeviceIdType.MESH
F32 = jnp.float32
BF16 = jnp.bfloat16

SIDE = 14
PADW = 16
HALF = SIDE // 2
SLOTS = 4
SROWS = SIDE * PADW
ROWS = SLOTS * SROWS
CW = 128
C = 512
HID = 512
NCHUNK = 8
CROWS = 128
NCHAN = 4
STATW = ROWS + CW


def aligned(value, step):
    return pl.multiple_of(value, step)


def dot(a, b, ca, cb):
    return lax.dot_general(a, b, (((ca,), (cb,)), ((), ())), preferred_element_type=F32)


def terms_of(values, terms):
    parts = []
    for _ in range(terms):
        part = values.astype(BF16)
        parts.append(part)
        values = values - part.astype(F32)
    return parts


def lane_sums(values, terms=2):
    ones = jnp.ones((8, values.shape[1]), BF16)
    total = None
    for part in terms_of(values, terms):
        here = dot(ones, part, 1, 1)
        total = here if total is None else total + here
    return total


def two_rows(first, second):
    row = lax.broadcasted_iota(jnp.int32, (8, first.shape[-1]), 0)
    return jnp.where(row == 0, first, jnp.where(row == 1, second, 0.0))


def two_columns(first, second):
    row = lax.broadcasted_iota(jnp.int32, (16, first.shape[-1]), 0)
    rows = jnp.zeros((16, first.shape[-1]), F32)
    for k, part in enumerate(terms_of(first, 3) + terms_of(second, 3)):
        rows = jnp.where(row == k, part.astype(F32), rows)
    row = lax.broadcasted_iota(jnp.int32, (16, 2 * CW), 0)
    lane = lax.broadcasted_iota(jnp.int32, (16, 2 * CW), 1)
    offset = row - jnp.where(lane < CW, 0, 3)
    pick = jnp.where((offset >= 0) & (offset < 3), 1.0, 0.0)
    both = dot(rows.astype(BF16), pick.astype(BF16), 0, 0)
    return both[:, :CW], both[:, CW:]


def kernel(t, hop, names, *refs):
    r = dict(zip(names, refs))
    first = t == 0
    peer = lax.axis_index("peer")
    chan = lax.axis_index("chan")
    my_z, my_y, my_x = peer % 4, (peer // 4) % 2, peer // 8
    core, side = chan % 2, chan // 2

    def at(new_peer, new_chan):
        return (new_peer, new_chan)

    c_core = side * 2 + 1 - core
    c_side = (1 - side) * 2 + core
    c_diag = (1 - side) * 2 + 1 - core
    d_core, d_side, d_diag = at(peer, c_core), at(peer, c_side), at(peer, c_diag)
    bit = (peer // (2**hop)) % 2
    d_hop = at(peer + (1 - 2 * bit) * (2**hop), chan)
    mine = {"x": my_x, "y": my_y, "z": my_z}
    count_of = {"x": 4, "y": 2, "z": 4}
    stride_of = {"x": 8, "y": 4, "z": 1}
    to, source, line = {}, {}, {}
    for dim, n in count_of.items():
        to[dim] = [(mine[dim] + d) % n for d in range(1, n)]
        source[dim] = [(mine[dim] + n - d) % n for d in range(1, n)]
        line[dim] = [at(peer + (c - mine[dim]) * stride_of[dim], chan) for c in to[dim]]

    counters = {"remote": 0, "local": 0}
    ends = []

    def take(kind, n):
        start = counters[kind]
        counters[kind] += n
        return start

    def remote(src, dst, device, index):
        return pltpu.make_async_remote_copy(
            src_ref=src,
            dst_ref=dst,
            send_sem=r["send"].at[index],
            recv_sem=r["recv"].at[index],
            device_id=device,
            device_id_type=MESH,
        )

    def push(src, dst, device):
        copy = remote(src, dst, device, take("remote", 1))
        copy.start()
        ends.append(copy.wait_send)
        return copy

    def local(src, dst):
        copy = pltpu.make_async_copy(src, dst, r["local"].at[take("local", 1)])
        copy.start()
        return copy

    P2, Y2, G2, F2 = r["P2"], r["Y2"], r["G2"], r["F2"]
    PB, PP, YB, YP, W = r["PB"], r["PP"], r["YB"], r["YP"], r["W"]

    def piece(ref, i):
        return ref.at[i // 4, pl.ds(aligned((i % 4) * CROWS, CROWS), CROWS), :]

    if first:
        G = [[r["G%d%d" % (u, h)] for h in range(2)] for u in range(2)]
        plan = ("yzx", "yxz", "yzx", "yxz") if hop == 2 else ("zyx", "zyx", "yzx", "yzx")
        order = {(u, h): plan[2 * u + h] for u in range(2) for h in range(2)}

        def block(u, h, near, far):
            return G[u][h].at[pl.ds((near * count_of[order[u, h][1]] + far) * 2, 2)]

        def own_block(u, h):
            return block(u, h, mine[order[u, h][0]], mine[order[u, h][1]])

        img_in = {
            (u, h): local(r["images"].at[u, :, pl.ds(h * HALF, HALF)], own_block(u, h))
            for u in range(2)
            for h in range(2)
        }
    p_sem = take("local", NCHUNK)

    def p_load(i):
        return pltpu.make_async_copy(
            piece(r["pm"].at[0], i), piece(P2, i), r["local"].at[p_sem + i]
        )

    def start_p(i, carry):
        p_load(i).start()
        return carry

    lax.fori_loop(0, NCHUNK, start_p, 0)
    CF = r["CF"]
    my_lanes = pl.ds(aligned(chan * CW, CW), CW)
    side_lanes = pl.ds(aligned(c_side * CW, CW), CW)
    cot_in = local(r["cot"].at[t], CF.at[:, my_lanes])
    y_in = local(r["ym"].at[0], Y2)
    g_in = local(r["gm"].at[0], G2)

    count = r["counts"][0, t]

    def valid(s):
        return jnp.where(s < count, 1.0, 0.0).astype(F32)

    inv = 1.0 / jnp.full((1, CW), count.astype(F32))

    if first:
        IDV = r["IDV"]
        lane = lax.broadcasted_iota(jnp.int32, (8, 128), 1)
        row = lax.broadcasted_iota(jnp.int32, (8, 128), 0)
        tile = jnp.zeros((8, 128), jnp.int32)
        for u in range(2):
            for s in range(SLOTS):
                tile = jnp.where((row == u) & (lane == s), r["ids"][u, 0, s], tile)
        IDV[0, my_x] = tile
        IDV[1, my_z] = tile

    barrier = pltpu.get_barrier_semaphore()
    greet = [d_core, d_side, d_diag] + (line["y"] + line["z"] + line["x"] if first else [d_hop])
    for device in greet:
        pl.semaphore_signal(barrier, inc=1, device_id=device, device_id_type=MESH)
    pl.semaphore_wait(barrier, len(greet))

    small = [
        push(r["pc"], r["RPC"], d_hop),
        push(r["pb"], r["RPB"], d_hop),
        push(r["yc"], r["RYC"], d_hop),
        push(r["yb"], r["RYB"], d_hop),
    ]

    fetch = {}
    if first:
        fetch["ids"] = [
            push(IDV.at[k, mine[dim]], IDV.at[k, mine[dim]], d)
            for k, dim in enumerate("xz")
            for d in line[dim]
        ]

    def images_begin(u):
        for h in range(2):
            near, far, _ = order[u, h]
            img_in[u, h].wait()
            own = own_block(u, h)
            fetch["near", u, h] = [push(own, own, d) for d in line[near]]
            fetch["far", u, h] = [push(own, own, d) for d in line[far]]

    def images_second(u):
        for h in range(2):
            near, far, _ = order[u, h]
            for copy, place in zip(fetch["near", u, h], source[near]):
                copy.wait_recv()
                part = block(u, h, place, mine[far])
                fetch["far", u, h] += [push(part, part, d) for d in line[far]]

    def place_of(ident, dim):
        return (ident // (2 * stride_of[dim])) % count_of[dim]

    def images_third(u):
        for h in range(2):
            near, far, last = order[u, h]
            for copy in fetch["far", u, h]:
                copy.wait_recv()
            XS, XR = r["XS"], r["XR%d%d" % (u, h)]

            def wanted(c, s):
                ident = r["IDS"]["xz".index(last), c, u, s]
                row = place_of(ident, near) * count_of[far] + place_of(ident, far)
                return G[u][h][row * 2 + ident % 2]

            fetch["x", u, h] = []
            for j in range(3):
                for s in range(SLOTS):
                    XS[u, h, j, s] = wanted(to[last][j], s)
                fetch["x", u, h].append(push(XS.at[u, h, j], XR.at[mine[last]], line[last][j]))
            for s in range(SLOTS):
                XR[mine[last], s] = wanted(mine[last], s)

    def images_end(u):
        for h in range(2):
            for copy in fetch["x", u, h]:
                copy.wait_recv()

    def picked(u, h, s):
        return r["XR%d%d" % (u, h)][place_of(r["ids"][u, 0, s], order[u, h][2]), s]

    if first:
        images_begin(0)

    p_send = take("remote", NCHUNK)

    def p_copy(i):
        return remote(piece(PB, i), piece(PP, i), d_hop, p_send + i)

    def rows_of(i):
        return (i // 4, pl.ds(aligned((i % 4) * CROWS, CROWS), CROWS), slice(None))

    def send_p(i, carry):
        p_load(i).wait()
        PB[rows_of(i)] = P2[rows_of(i)].astype(BF16)
        p_copy(i).start()
        return carry

    lax.fori_loop(0, NCHUNK, send_p, 0)

    r["XP"][...] = jnp.zeros_like(r["XP"])
    cot_in.wait()
    cot_sum = jnp.zeros((1, CW), F32)
    for s in range(SLOTS):
        rows = slice(s * SROWS, (s + 1) * SROWS)
        live = CF[rows, my_lanes].astype(F32) * valid(s)
        CF[rows, my_lanes] = live.astype(BF16)
        cot_sum = cot_sum + jnp.sum(live, 0, keepdims=True)
    cot_core = push(CF.at[:, my_lanes], CF.at[:, my_lanes], d_core)
    cot_side = push(CF.at[:, my_lanes], CF.at[:, my_lanes], d_side)

    for copy in small:
        copy.wait_recv()
    qc, qb = r["qc"], r["qb"]
    qc[...] = 0.5 * (r["pc"][...] + r["RPC"][...]) - LEARNING_RATE * r["yc"][...]
    qb[...] = 0.5 * (r["pb"][...] + r["RPB"][...]) - LEARNING_RATE * r["yb"][...]

    def chan_row(k):
        return qc[k]

    if first:
        images_second(0)
        for copy in fetch["ids"]:
            copy.wait_recv()
        ids_in = local(IDV, r["IDS"])
        ids_in.wait()
        images_third(0)
        images_begin(1)
        images_end(0)

    XP, SH, X = r["XP"], r["SH"], r["X"]
    for s in range(SLOTS):
        for h in range(2):
            image = picked(0, h, s) if first else r["picked"][s, h * HALF : (h + 1) * HALF]
            top = 3 + h * HALF
            XP[s, top : top + HALF, 3 : 3 + PADW, :] = image.astype(F32) * valid(s)

    def shift(s, carry):
        for v in range(KS):
            SH[v, s] = XP[s, :, v : v + PADW, :]
        return carry

    lax.fori_loop(0, SLOTS, shift, 0)

    def conv_slot(s, carry):
        def column(v, acc):
            for u in range(KS):
                acc = acc + SH[v, s, u : u + SIDE] * qc[u * KS + v]
            return acc

        acc = lax.fori_loop(0, KS, column, jnp.zeros((SIDE, PADW, CW), F32))
        X[pl.ds(aligned(s * SROWS, SROWS), SROWS), :] = acc.reshape(SROWS, CW) + chan_row(TAPS)
        return carry

    lax.fori_loop(0, SLOTS, conv_slot, 0)

    STR = r["STR"]
    conv_out = X[...]
    mean_here = jnp.sum(conv_out, 1, keepdims=True) * (1.0 / CW)
    centred = conv_out - mean_here
    mean_row = lane_sums(conv_out, 3) * (1.0 / CW)
    STR[chan, :, 0:ROWS] = two_rows(mean_row, lane_sums(centred * centred))
    STR[chan, :, ROWS:STATW] = jnp.broadcast_to(chan_row(TAPS + 4), (8, CW))
    stats = [push(STR.at[chan], STR.at[chan], d) for d in (d_core, d_side, d_diag)]
    cot_side.wait_recv()
    cot_far = push(CF.at[:, side_lanes], CF.at[:, side_lanes], d_core)
    for copy in stats:
        copy.wait_recv()
    means = [STR[j, 0:1, 0:ROWS] for j in range(NCHAN)]
    mean = (means[0] + means[1] + means[2] + means[3]) * 0.25
    squares = STR[0, 1:2, 0:ROWS] + STR[1, 1:2, 0:ROWS] + STR[2, 1:2, 0:ROWS] + STR[3, 1:2, 0:ROWS]
    for j in range(NCHAN):
        squares = squares + CW * (means[j] - mean) * (means[j] - mean)
    deviation = lax.rsqrt(squares * (1.0 / C) + EPS)
    mean_col, inv_col = two_columns(mean, deviation)
    r["INV"][...] = inv_col
    xhat = (X[...] - mean_col) * inv_col
    X[...] = xhat
    NF = r["NF"]
    NF[:, my_lanes] = (xhat * chan_row(TAPS + 1) + chan_row(TAPS + 2)).astype(BF16)

    na, nb, nc = take("remote", SLOTS), take("remote", SLOTS), take("remote", SLOTS)

    def slot_rows(s):
        return pl.ds(aligned(s * SROWS, SROWS), SROWS)

    def norm_core(s):
        part = NF.at[slot_rows(s), my_lanes]
        return remote(part, part, d_core, na + s)

    def norm_side(s):
        part = NF.at[slot_rows(s), my_lanes]
        return remote(part, part, d_side, nb + s)

    def norm_far(s):
        part = NF.at[slot_rows(s), side_lanes]
        return remote(part, part, d_core, nc + s)

    def norm_send(s, carry):
        norm_side(s).start()
        norm_core(s).start()
        return carry

    lax.fori_loop(0, SLOTS, norm_send, 0)

    if first:
        images_second(1)

    cot_core.wait_recv()
    cot_far.wait_recv()
    DB = r["DB"]
    for j in range(NCHAN):
        lanes = slice(j * CW, (j + 1) * CW)
        factor = inv * STR[j, 0:1, ROWS:STATW]
        DB[:, lanes] = (CF[:, lanes].astype(F32) * factor).astype(BF16)

    y_in.wait()

    def mix(i, carry):
        p_copy(i).wait_recv()
        q = 0.5 * (P2[rows_of(i)] + PP[rows_of(i)].astype(F32)) - LEARNING_RATE * Y2[rows_of(i)]
        P2[rows_of(i)] = q
        W[rows_of(i)] = q.astype(BF16)
        return carry

    lax.fori_loop(0, NCHUNK, mix, 0)
    q_out = local(P2, r["qm"].at[0])

    y_send = take("remote", NCHUNK)

    def y_copy(i):
        return remote(piece(YB, i), piece(YP, i), d_hop, y_send + i)

    def send_y(i, carry):
        YB[rows_of(i)] = Y2[rows_of(i)].astype(BF16)
        y_copy(i).start()
        return carry

    if hop != 2:
        lax.fori_loop(0, NCHUNK, send_y, 0)

    if first:
        images_third(1)

    ACT, DH, DP, R1, S2, R2, DN = (r[n] for n in ("ACT", "DH", "DP", "R1", "S2", "R2", "DN"))
    r1, r2 = take("remote", 2 * SLOTS), take("remote", SLOTS)

    def near_copy(s, b):
        lanes = pl.ds(aligned((b * 2 + 1 - core) * CW, CW), CW)
        return remote(DP.at[slot_rows(s), lanes], R1.at[b, slot_rows(s)], d_core, r1 + 2 * s + b)

    def far_copy(s):
        return remote(S2.at[slot_rows(s)], R2.at[slot_rows(s)], d_side, r2 + s)

    GB = r["GB"]
    GB[...] = jnp.zeros_like(GB)

    def slot_step(step, carry):
        if hop == 2:
            send_y(step, carry)

        @pl.when(step < SLOTS)
        def _():
            norm_side(step).wait_recv()
            norm_far(step).start()

        @pl.when((step > 0) & (step <= SLOTS))
        def _():
            s = step - 1
            norm_core(s).wait_recv()
            norm_far(s).wait_recv()
            rows = slot_rows(s)
            hidden = dot(NF[rows, :], W[0], 1, 0) + qb[...]
            cdf = 0.5 * (1.0 + lax.erf(hidden * 0.7071067811865476))
            density = jnp.exp(-0.5 * hidden * hidden) * 0.3989422804014327
            ACT[rows, :] = (hidden * cdf).astype(BF16)
            slope = cdf + hidden * density
            dhidden = dot(DB[rows, :], W[1], 1, 0) * slope
            GB[...] += jnp.sum(dhidden, 0, keepdims=True)
            low = dhidden.astype(BF16)
            DH[rows, :] = low
            DP[rows, :] = dot(low, W[0], 1, 1)
            near_copy(s, 0).start()
            near_copy(s, 1).start()

        @pl.when(step > 1)
        def _():
            s = step - 2
            rows = slot_rows(s)
            near_copy(s, 0).wait_recv()
            near_copy(s, 1).wait_recv()
            S2[rows, :] = (DP[rows, side_lanes] + R1[1 - side, rows, :]).astype(BF16)
            far_copy(s).start()
            DN[rows, :] = DP[rows, my_lanes] + R1[side, rows, :]

        return carry

    lax.fori_loop(0, SLOTS + 2, slot_step, 0)
    if hop == 2:
        lax.fori_loop(SLOTS + 2, NCHUNK, send_y, 0)

    BS, BR, GS = r["BS"], r["BR"], r["GS"]

    def scale_part(j, carry):
        lanes = pl.ds(aligned(j * CW, CW), CW)
        rows = pl.ds(aligned(j * CW, CW), CW)
        pair = dot(CF[:, lanes], ACT[...], 0, 0)
        weight = W[1, rows, :].astype(F32)
        GS[j] = lane_sums(pair * weight)
        return carry

    lax.fori_loop(0, NCHAN, scale_part, 0)

    def far_wait(s, carry):
        far_copy(s).wait_recv()
        return carry

    lax.fori_loop(0, SLOTS, far_wait, 0)
    dnormed = DN[...] + R2[...].astype(F32)
    DN[...] = dnormed
    xhat = X[...]
    dxhat = dnormed * chan_row(TAPS + 1)
    sums = two_rows(lane_sums(dxhat), lane_sums(dxhat * xhat))
    for j in range(NCHAN):
        BS[j, :, 0:ROWS] = sums
        BS[j, :, ROWS:STATW] = GS[j]
    BR[chan] = BS[chan]
    back = [
        push(BS.at[c], BR.at[chan], d)
        for c, d in ((c_core, d_core), (c_side, d_side), (c_diag, d_diag))
    ]

    def mats_part(j, carry):
        lanes = pl.ds(aligned(j * CW, CW), CW)
        F2[0, lanes, :] = dot(NF[:, lanes], DH[...], 0, 0)
        F2[1, lanes, :] = dot(DB[:, lanes], ACT[...], 0, 0)
        return carry

    lax.fori_loop(0, NCHAN, mats_part, 0)
    if first:
        f_out = local(F2, r["fm"].at[0])

    for copy in back:
        copy.wait_recv()
    totals = BR[0] + BR[1] + BR[2] + BR[3]
    mean_a, mean_b = two_columns(
        totals[0:1, 0:ROWS] * (1.0 / C), totals[1:2, 0:ROWS] * (1.0 / C)
    )
    dnormed = DN[...]
    xhat = X[...]
    dconv = (dnormed * chan_row(TAPS + 1) - mean_a - xhat * mean_b) * r["INV"][...]
    DC, FC = r["DC"], r["FC"]
    DC[...] = dconv.reshape(SLOTS, SIDE, PADW, CW)
    FC[TAPS] = jnp.sum(dconv, 0, keepdims=True)
    FC[TAPS + 1] = jnp.sum(dnormed * xhat, 0, keepdims=True)
    FC[TAPS + 2] = jnp.sum(dnormed, 0, keepdims=True)
    FC[TAPS + 3] = chan_row(TAPS + 4) * inv * cot_sum
    FC[TAPS + 4] = inv * (totals[0:1, ROWS:STATW] + chan_row(TAPS + 3) * cot_sum)

    def tap_column(v, carry):
        def over(s, accs):
            grad = DC[s]
            return tuple(
                accs[u] + jnp.sum(SH[v, s, u : u + SIDE] * grad, 0) for u in range(KS)
            )

        accs = lax.fori_loop(0, SLOTS, over, tuple(jnp.zeros((PADW, CW), F32) for _ in range(KS)))
        for u in range(KS):
            FC[u * KS + v] = jnp.sum(accs[u], 0, keepdims=True)
        return carry

    lax.fori_loop(0, KS, tap_column, 0)

    fresh = FC[...]
    r["new_yc"][...] = 0.5 * (r["yc"][...] + r["RYC"][...]) + fresh - r["gc"][...]
    r["new_yb"][...] = 0.5 * (r["yb"][...] + r["RYB"][...]) + GB[...] - r["gb"][...]
    if first:
        r["fc"][...] = fresh
        r["fb"][...] = GB[...]
        images_end(1)
        for s in range(SLOTS):
            for h in range(2):
                r["picked_next"][s, h * HALF : (h + 1) * HALF] = picked(1, h, s)

    g_in.wait()
    out_sem = take("local", NCHUNK)

    def y_out(i):
        return pltpu.make_async_copy(
            piece(Y2, i), piece(r["new_ym"].at[0], i), r["local"].at[out_sem + i]
        )

    def track(i, carry):
        y_copy(i).wait_recv()
        at_i = rows_of(i)
        Y2[at_i] = 0.5 * (Y2[at_i] + YP[at_i].astype(F32)) + F2[at_i] - G2[at_i]
        y_out(i).start()
        return carry

    lax.fori_loop(0, NCHUNK, track, 0)

    def swaps_end(i, carry):
        p_copy(i).wait_send()
        y_copy(i).wait_send()
        y_out(i).wait()
        return carry

    lax.fori_loop(0, NCHUNK, swaps_end, 0)

    def slots_end(s, carry):
        norm_core(s).wait_send()
        norm_side(s).wait_send()
        norm_far(s).wait_send()
        near_copy(s, 0).wait_send()
        near_copy(s, 1).wait_send()
        far_copy(s).wait_send()
        return carry

    lax.fori_loop(0, SLOTS, slots_end, 0)
    for wait in ends:
        wait()
    q_out.wait()
    if first:
        f_out.wait()


def iteration(t, hop, state, images, cot, ids, counts):
    first = t == 0
    pm, pc, pb, ym, yc, yb, gm, gc, gb = state
    hbm = pl.BlockSpec(memory_space=pl.ANY)
    vmem = pl.BlockSpec(memory_space=pltpu.VMEM)
    smem = pl.BlockSpec(memory_space=pltpu.SMEM)
    ins = [("images", images, hbm), ("ids", ids, smem)] if first else [("picked", images, vmem)]
    ins += [("counts", counts, smem), ("cot", cot, hbm)]
    ins += [("pm", pm, hbm), ("pc", pc, vmem), ("pb", pb, vmem)]
    ins += [("ym", ym, hbm), ("yc", yc, vmem), ("yb", yb, vmem)]
    ins += [("gm", gm, hbm), ("gc", gc, vmem), ("gb", gb, vmem)]
    outs = [("qm", pm, hbm), ("qc", pc, vmem), ("qb", pb, vmem)]
    outs += [("new_ym", ym, hbm), ("new_yc", yc, vmem), ("new_yb", yb, vmem)]
    if first:
        outs += [("fm", gm, hbm), ("fc", gc, vmem), ("fb", gb, vmem)]
        outs += [("picked_next", jax.ShapeDtypeStruct((SLOTS, SIDE, PADW, CW), BF16), vmem)]
    V = pltpu.VMEM
    mats = (2, C, HID)
    half = (HALF, PADW, CW)
    scratch = {n: V(mats, F32) for n in ("P2", "Y2", "G2", "F2")}
    scratch |= {n: V(mats, BF16) for n in ("PB", "PP", "YB", "YP", "W")}
    scratch |= {n: V((ROWS, C), BF16) for n in ("NF", "CF", "DB", "ACT", "DH")}
    scratch |= {n: V((ROWS, CW), F32) for n in ("X", "INV", "DN")}
    scratch |= {n: V((ROWS, CW), BF16) for n in ("S2", "R2")}
    scratch |= {n: V((SLOTS, SIDE, PADW, CW), F32) for n in ("DC",)}
    scratch |= {n: V((NCHAN, 8, STATW), F32) for n in ("STR", "BS", "BR")}
    scratch |= {n: V((TAPS + 5, 1, CW), F32) for n in ("RPC", "RYC", "FC")}
    scratch |= {n: V((1, HID), F32) for n in ("RPB", "RYB", "GB")}
    scratch |= {
        "DP": V((ROWS, C), F32),
        "R1": V((2, ROWS, CW), F32),
        "GS": V((NCHAN, 8, CW), F32),
        "XP": V((SLOTS, SIDE + 6, 24, CW), F32),
        "SH": V((KS, SLOTS, SIDE + 6, PADW, CW), F32),
        "send": pltpu.SemaphoreType.DMA((128,)),
        "recv": pltpu.SemaphoreType.DMA((128,)),
        "local": pltpu.SemaphoreType.DMA((32,)),
    }
    if first:
        for u in range(2):
            for h in range(2):
                scratch["G%d%d" % (u, h)] = V((16,) + half, BF16)
                scratch["XR%d%d" % (u, h)] = V((4, SLOTS) + half, BF16)
        scratch |= {
            "XS": V((2, 2, 3, SLOTS) + half, BF16),
            "IDV": V((2, 4, 8, 128), jnp.int32),
            "IDS": pltpu.SMEM((2, 4, 8, 128), jnp.int32),
        }
    names = [n for n, _, _ in ins] + [n for n, _, _ in outs] + list(scratch)
    return pl.pallas_call(
        functools.partial(kernel, t, hop, names),
        out_shape=[jax.ShapeDtypeStruct(a.shape, a.dtype) for _, a, _ in outs],
        in_specs=[s for _, _, s in ins],
        out_specs=[s for _, _, s in outs],
        scratch_shapes=list(scratch.values()),
        compiler_params=pltpu.CompilerParams(
            collective_id=t * 3 + hop,
            has_side_effects=True,
            vmem_limit_bytes=58 * 1024 * 1024,
        ),
    )(*[a for _, a, _ in ins])


def copies(*refs):
    n = len(refs) // 2
    started = [pltpu.make_async_copy(refs[i], refs[n + i], refs[2 * n].at[i]) for i in range(n)]
    for copy in started:
        copy.start()
    for copy in started:
        copy.wait()


def handed_on(values):
    hbm = pl.BlockSpec(memory_space=pl.ANY)
    return pl.pallas_call(
        copies,
        out_shape=[jax.ShapeDtypeStruct(a.shape, a.dtype) for a in values],
        in_specs=[hbm] * len(values),
        out_specs=[hbm] * len(values),
        scratch_shapes=[pltpu.SemaphoreType.DMA((len(values),))],
    )(*values)


def on_device(images, cotangent, image_ids, counts, hop_exponents, *state):
    def padded(maps):
        return jnp.pad(maps, ((0, 0), (0, 0), (0, 0), (0, PADW - SIDE), (0, 0)))

    images = padded(images)
    cot = padded(cotangent[:, 0]).reshape(ITERS, ROWS, CW)
    counts = counts.T

    def turned(values):
        return tuple(a.transpose(1, 0, 2) if i % 3 == 1 else a for i, a in enumerate(values))

    def branch(t, hop):
        def run(operands):
            source, state = operands
            return iteration(t, hop, state, source, cot, image_ids, counts)

        return run

    def step(t, source, state):
        return lax.switch(
            hop_exponents[t], [branch(t, hop) for hop in range(3)], (source, state)
        )

    out = step(0, images, turned(state))
    return turned(handed_on(step(1, out[9], tuple(out[:9]))))


def solution(mesh):
    mats, chans, bias = P("peer", None, None, "chan"), P("peer", None, "chan"), P("peer", "chan")
    in_specs = (
        P(None, "peer", None, None, "chan"),
        P(None, "peer", None, None, None, "chan"),
        P(None, "peer", None),
        P(None, "peer"),
        P(),
    ) + (mats, chans, bias) * 3
    return jax.shard_map(
        on_device, mesh=mesh, in_specs=in_specs, out_specs=(mats, chans, bias) * 2, check_vma=False
    )
```

```python
import functools

import jax
import jax.numpy as jnp
from jax import lax
from jax.experimental import pallas as pl
from jax.experimental.pallas import tpu as pltpu
from jax.sharding import PartitionSpec as P

KS = 7
TAPS = KS * KS
ITERS = 2
EPS = 1e-06
LEARNING_RATE = 0.01
MESH = pl.DeviceIdType.MESH
F32 = jnp.float32
BF16 = jnp.bfloat16

SIDE = 14
PADW = 16
HALF = SIDE // 2
SLOTS = 4
SROWS = SIDE * PADW
ROWS = SLOTS * SROWS
CW = 128
C = 512
HID = 512
NCHUNK = 8
CROWS = 128
NCHAN = 4
STATW = ROWS + CW


def aligned(value, step):
    return pl.multiple_of(value, step)


def dot(a, b, ca, cb):
    return lax.dot_general(a, b, (((ca,), (cb,)), ((), ())), preferred_element_type=F32)


def terms_of(values, terms):
    parts = []
    for _ in range(terms):
        part = values.astype(BF16)
        parts.append(part)
        values = values - part.astype(F32)
    return parts


def lane_sums(values, terms=2):
    ones = jnp.ones((8, values.shape[1]), BF16)
    total = None
    for part in terms_of(values, terms):
        here = dot(ones, part, 1, 1)
        total = here if total is None else total + here
    return total


def two_rows(first, second):
    row = lax.broadcasted_iota(jnp.int32, (8, first.shape[-1]), 0)
    return jnp.where(row == 0, first, jnp.where(row == 1, second, 0.0))


def two_columns(first, second):
    row = lax.broadcasted_iota(jnp.int32, (16, first.shape[-1]), 0)
    rows = jnp.zeros((16, first.shape[-1]), F32)
    for k, part in enumerate(terms_of(first, 3) + terms_of(second, 3)):
        rows = jnp.where(row == k, part.astype(F32), rows)
    row = lax.broadcasted_iota(jnp.int32, (16, 2 * CW), 0)
    lane = lax.broadcasted_iota(jnp.int32, (16, 2 * CW), 1)
    offset = row - jnp.where(lane < CW, 0, 3)
    pick = jnp.where((offset >= 0) & (offset < 3), 1.0, 0.0)
    both = dot(rows.astype(BF16), pick.astype(BF16), 0, 0)
    return both[:, :CW], both[:, CW:]


def kernel(t, hop, names, *refs):
    r = dict(zip(names, refs))
    first = t == 0
    peer = lax.axis_index("peer")
    chan = lax.axis_index("chan")
    my_z, my_y, my_x = peer % 4, (peer // 4) % 2, peer // 8
    core, side = chan % 2, chan // 2

    def at(new_peer, new_chan):
        return (new_peer, new_chan)

    c_core = side * 2 + 1 - core
    c_side = (1 - side) * 2 + core
    c_diag = (1 - side) * 2 + 1 - core
    d_core, d_side, d_diag = at(peer, c_core), at(peer, c_side), at(peer, c_diag)
    bit = (peer // (2**hop)) % 2
    d_hop = at(peer + (1 - 2 * bit) * (2**hop), chan)
    mine = {"x": my_x, "y": my_y, "z": my_z}
    count_of = {"x": 4, "y": 2, "z": 4}
    stride_of = {"x": 8, "y": 4, "z": 1}
    to, source, line = {}, {}, {}
    for dim, n in count_of.items():
        to[dim] = [(mine[dim] + d) % n for d in range(1, n)]
        source[dim] = [(mine[dim] + n - d) % n for d in range(1, n)]
        line[dim] = [at(peer + (c - mine[dim]) * stride_of[dim], chan) for c in to[dim]]

    counters = {"remote": 0, "local": 0}
    ends = []

    def take(kind, n):
        start = counters[kind]
        counters[kind] += n
        return start

    def remote(src, dst, device, index):
        return pltpu.make_async_remote_copy(
            src_ref=src,
            dst_ref=dst,
            send_sem=r["send"].at[index],
            recv_sem=r["recv"].at[index],
            device_id=device,
            device_id_type=MESH,
        )

    def push(src, dst, device):
        copy = remote(src, dst, device, take("remote", 1))
        copy.start()
        ends.append(copy.wait_send)
        return copy

    def local(src, dst):
        copy = pltpu.make_async_copy(src, dst, r["local"].at[take("local", 1)])
        copy.start()
        return copy

    P2, Y2, G2, F2 = r["P2"], r["Y2"], r["G2"], r["F2"]
    PB, PP, YB, YP, W = r["PB"], r["PP"], r["YB"], r["YP"], r["W"]

    def piece(ref, i):
        return ref.at[i // 4, pl.ds(aligned((i % 4) * CROWS, CROWS), CROWS), :]

    if first:
        G = [[r["G%d%d" % (u, h)] for h in range(2)] for u in range(2)]
        plan = ("yzx", "yxz") if hop == 2 else ("zyx", "zyx")
        order = {(u, h): plan[h] for u in range(2) for h in range(2)}

        def block(u, h, near, far):
            return G[u][h].at[pl.ds((near * count_of[order[u, h][1]] + far) * 2, 2)]

        def own_block(u, h):
            return block(u, h, mine[order[u, h][0]], mine[order[u, h][1]])

        img_in = {
            (u, h): local(r["images"].at[u, :, pl.ds(h * HALF, HALF)], own_block(u, h))
            for u in range(2)
            for h in range(2)
        }
    p_sem = take("local", NCHUNK)

    def p_load(i):
        return pltpu.make_async_copy(
            piece(r["pm"].at[0], i), piece(P2, i), r["local"].at[p_sem + i]
        )

    def start_p(i, carry):
        p_load(i).start()
        return carry

    lax.fori_loop(0, NCHUNK, start_p, 0)
    CF = r["CF"]
    my_lanes = pl.ds(aligned(chan * CW, CW), CW)
    side_lanes = pl.ds(aligned(c_side * CW, CW), CW)
    cot_in = local(r["cot"].at[t], CF.at[:, my_lanes])
    y_in = local(r["ym"].at[0], Y2)
    g_in = local(r["gm"].at[0], G2)

    count = r["counts"][0, t]

    def valid(s):
        return jnp.where(s < count, 1.0, 0.0).astype(F32)

    inv = 1.0 / jnp.full((1, CW), count.astype(F32))

    if first:
        IDV = r["IDV"]
        lane = lax.broadcasted_iota(jnp.int32, (8, 128), 1)
        row = lax.broadcasted_iota(jnp.int32, (8, 128), 0)
        tile = jnp.zeros((8, 128), jnp.int32)
        for u in range(2):
            for s in range(SLOTS):
                tile = jnp.where((row == u) & (lane == s), r["ids"][u, 0, s], tile)
        IDV[0, my_x] = tile
        IDV[1, my_z] = tile

    barrier = pltpu.get_barrier_semaphore()
    greet = [d_core, d_side, d_diag] + (line["y"] + line["z"] + line["x"] if first else [d_hop])
    for device in greet:
        pl.semaphore_signal(barrier, inc=1, device_id=device, device_id_type=MESH)
    pl.semaphore_wait(barrier, len(greet))

    small = [
        push(r["pc"], r["RPC"], d_hop),
        push(r["pb"], r["RPB"], d_hop),
        push(r["yc"], r["RYC"], d_hop),
        push(r["yb"], r["RYB"], d_hop),
    ]

    fetch = {}
    if first:
        fetch["ids"] = [
            push(IDV.at[k, mine[dim]], IDV.at[k, mine[dim]], d)
            for k, dim in enumerate("xz")
            for d in line[dim]
        ]

    def images_begin(u):
        for h in range(2):
            near, far, _ = order[u, h]
            img_in[u, h].wait()
            own = own_block(u, h)
            fetch["near", u, h] = [push(own, own, d) for d in line[near]]
            fetch["far", u, h] = [push(own, own, d) for d in line[far]]

    def images_second(u):
        for h in range(2):
            near, far, _ = order[u, h]
            for copy, place in zip(fetch["near", u, h], source[near]):
                copy.wait_recv()
                part = block(u, h, place, mine[far])
                fetch["far", u, h] += [push(part, part, d) for d in line[far]]

    def place_of(ident, dim):
        return (ident // (2 * stride_of[dim])) % count_of[dim]

    def images_third(u):
        for h in range(2):
            near, far, last = order[u, h]
            for copy in fetch["far", u, h]:
                copy.wait_recv()
            XS, XR = r["XS"], r["XR%d%d" % (u, h)]

            def wanted(c, s):
                ident = r["IDS"]["xz".index(last), c, u, s]
                row = place_of(ident, near) * count_of[far] + place_of(ident, far)
                return G[u][h][row * 2 + ident % 2]

            fetch["x", u, h] = []
            for j in range(3):
                for s in range(SLOTS):
                    XS[u, h, j, s] = wanted(to[last][j], s)
                fetch["x", u, h].append(push(XS.at[u, h, j], XR.at[mine[last]], line[last][j]))
            for s in range(SLOTS):
                XR[mine[last], s] = wanted(mine[last], s)

    def images_end(u):
        for h in range(2):
            for copy in fetch["x", u, h]:
                copy.wait_recv()

    def picked(u, h, s):
        return r["XR%d%d" % (u, h)][place_of(r["ids"][u, 0, s], order[u, h][2]), s]

    if first:
        images_begin(0)

    p_send = take("remote", NCHUNK)

    def p_copy(i):
        return remote(piece(PB, i), piece(PP, i), d_hop, p_send + i)

    def rows_of(i):
        return (i // 4, pl.ds(aligned((i % 4) * CROWS, CROWS), CROWS), slice(None))

    def send_p(i, carry):
        p_load(i).wait()
        PB[rows_of(i)] = P2[rows_of(i)].astype(BF16)
        p_copy(i).start()
        return carry

    lax.fori_loop(0, NCHUNK, send_p, 0)

    r["XP"][...] = jnp.zeros_like(r["XP"])
    cot_in.wait()
    cot_sum = jnp.zeros((1, CW), F32)
    for s in range(SLOTS):
        rows = slice(s * SROWS, (s + 1) * SROWS)
        live = CF[rows, my_lanes].astype(F32) * valid(s)
        CF[rows, my_lanes] = live.astype(BF16)
        cot_sum = cot_sum + jnp.sum(live, 0, keepdims=True)
    cot_core = push(CF.at[:, my_lanes], CF.at[:, my_lanes], d_core)
    cot_side = push(CF.at[:, my_lanes], CF.at[:, my_lanes], d_side)

    for copy in small:
        copy.wait_recv()
    qc, qb = r["qc"], r["qb"]
    qc[...] = 0.5 * (r["pc"][...] + r["RPC"][...]) - LEARNING_RATE * r["yc"][...]
    qb[...] = 0.5 * (r["pb"][...] + r["RPB"][...]) - LEARNING_RATE * r["yb"][...]

    def chan_row(k):
        return qc[k]

    if first:
        images_second(0)
        for copy in fetch["ids"]:
            copy.wait_recv()
        ids_in = local(IDV, r["IDS"])
        ids_in.wait()
        images_third(0)
        images_end(0)
        images_begin(1)

    XP, SH, X = r["XP"], r["SH"], r["X"]
    for s in range(SLOTS):
        for h in range(2):
            image = picked(0, h, s) if first else r["picked"][s, h * HALF : (h + 1) * HALF]
            top = 3 + h * HALF
            XP[s, top : top + HALF, 3 : 3 + PADW, :] = image.astype(F32) * valid(s)

    def shift(s, carry):
        for v in range(KS):
            SH[v, s] = XP[s, :, v : v + PADW, :]
        return carry

    lax.fori_loop(0, SLOTS, shift, 0)

    def conv_slot(s, carry):
        def column(v, acc):
            for u in range(KS):
                acc = acc + SH[v, s, u : u + SIDE] * qc[u * KS + v]
            return acc

        acc = lax.fori_loop(0, KS, column, jnp.zeros((SIDE, PADW, CW), F32))
        X[pl.ds(aligned(s * SROWS, SROWS), SROWS), :] = acc.reshape(SROWS, CW) + chan_row(TAPS)
        return carry

    lax.fori_loop(0, SLOTS, conv_slot, 0)

    STR = r["STR"]
    conv_out = X[...]
    mean_here = jnp.sum(conv_out, 1, keepdims=True) * (1.0 / CW)
    centred = conv_out - mean_here
    mean_row = lane_sums(conv_out, 3) * (1.0 / CW)
    STR[chan, :, 0:ROWS] = two_rows(mean_row, lane_sums(centred * centred))
    STR[chan, :, ROWS:STATW] = jnp.broadcast_to(chan_row(TAPS + 4), (8, CW))
    stats = [push(STR.at[chan], STR.at[chan], d) for d in (d_core, d_side, d_diag)]
    cot_side.wait_recv()
    cot_far = push(CF.at[:, side_lanes], CF.at[:, side_lanes], d_core)
    for copy in stats:
        copy.wait_recv()
    means = [STR[j, 0:1, 0:ROWS] for j in range(NCHAN)]
    mean = (means[0] + means[1] + means[2] + means[3]) * 0.25
    squares = STR[0, 1:2, 0:ROWS] + STR[1, 1:2, 0:ROWS] + STR[2, 1:2, 0:ROWS] + STR[3, 1:2, 0:ROWS]
    for j in range(NCHAN):
        squares = squares + CW * (means[j] - mean) * (means[j] - mean)
    deviation = lax.rsqrt(squares * (1.0 / C) + EPS)
    mean_col, inv_col = two_columns(mean, deviation)
    r["INV"][...] = inv_col
    xhat = (X[...] - mean_col) * inv_col
    X[...] = xhat
    NF = r["NF"]
    NF[:, my_lanes] = (xhat * chan_row(TAPS + 1) + chan_row(TAPS + 2)).astype(BF16)

    na, nb, nc = take("remote", SLOTS), take("remote", SLOTS), take("remote", SLOTS)

    def slot_rows(s):
        return pl.ds(aligned(s * SROWS, SROWS), SROWS)

    def norm_core(s):
        part = NF.at[slot_rows(s), my_lanes]
        return remote(part, part, d_core, na + s)

    def norm_side(s):
        part = NF.at[slot_rows(s), my_lanes]
        return remote(part, part, d_side, nb + s)

    def norm_far(s):
        part = NF.at[slot_rows(s), side_lanes]
        return remote(part, part, d_core, nc + s)

    def norm_send(s, carry):
        norm_side(s).start()
        norm_core(s).start()
        return carry

    lax.fori_loop(0, SLOTS, norm_send, 0)

    if first:
        images_second(1)

    cot_core.wait_recv()
    cot_far.wait_recv()
    DB = r["DB"]
    for j in range(NCHAN):
        lanes = slice(j * CW, (j + 1) * CW)
        factor = inv * STR[j, 0:1, ROWS:STATW]
        DB[:, lanes] = (CF[:, lanes].astype(F32) * factor).astype(BF16)

    y_in.wait()

    def mix(i, carry):
        p_copy(i).wait_recv()
        q = 0.5 * (P2[rows_of(i)] + PP[rows_of(i)].astype(F32)) - LEARNING_RATE * Y2[rows_of(i)]
        P2[rows_of(i)] = q
        W[rows_of(i)] = q.astype(BF16)
        return carry

    lax.fori_loop(0, NCHUNK, mix, 0)
    q_out = local(P2, r["qm"].at[0])

    y_send = take("remote", NCHUNK)

    def y_copy(i):
        return remote(piece(YB, i), piece(YP, i), d_hop, y_send + i)

    def send_y(i, carry):
        YB[rows_of(i)] = Y2[rows_of(i)].astype(BF16)
        y_copy(i).start()
        return carry

    if hop != 2:
        lax.fori_loop(0, NCHUNK, send_y, 0)

    ACT, DH, DP, R1, S2, R2, DN = (r[n] for n in ("ACT", "DH", "DP", "R1", "S2", "R2", "DN"))
    r1, r2 = take("remote", 2 * SLOTS), take("remote", SLOTS)

    def near_copy(s, b):
        lanes = pl.ds(aligned((b * 2 + 1 - core) * CW, CW), CW)
        return remote(DP.at[slot_rows(s), lanes], R1.at[b, slot_rows(s)], d_core, r1 + 2 * s + b)

    def far_copy(s):
        return remote(S2.at[slot_rows(s)], R2.at[slot_rows(s)], d_side, r2 + s)

    GB = r["GB"]
    GB[...] = jnp.zeros_like(GB)

    def slot_step(step, carry):
        if hop == 2:
            send_y(step, carry)

        @pl.when(step < SLOTS)
        def _():
            norm_side(step).wait_recv()
            norm_far(step).start()

        @pl.when((step > 0) & (step <= SLOTS))
        def _():
            s = step - 1
            norm_core(s).wait_recv()
            norm_far(s).wait_recv()
            rows = slot_rows(s)
            hidden = dot(NF[rows, :], W[0], 1, 0) + qb[...]
            cdf = 0.5 * (1.0 + lax.erf(hidden * 0.7071067811865476))
            density = jnp.exp(-0.5 * hidden * hidden) * 0.3989422804014327
            ACT[rows, :] = (hidden * cdf).astype(BF16)
            slope = cdf + hidden * density
            dhidden = dot(DB[rows, :], W[1], 1, 0) * slope
            GB[...] += jnp.sum(dhidden, 0, keepdims=True)
            low = dhidden.astype(BF16)
            DH[rows, :] = low
            DP[rows, :] = dot(low, W[0], 1, 1)
            near_copy(s, 0).start()
            near_copy(s, 1).start()

        @pl.when(step > 1)
        def _():
            s = step - 2
            rows = slot_rows(s)
            near_copy(s, 0).wait_recv()
            near_copy(s, 1).wait_recv()
            S2[rows, :] = (DP[rows, side_lanes] + R1[1 - side, rows, :]).astype(BF16)
            far_copy(s).start()
            DN[rows, :] = DP[rows, my_lanes] + R1[side, rows, :]

        return carry

    lax.fori_loop(0, SLOTS + 2, slot_step, 0)
    if hop == 2:
        lax.fori_loop(SLOTS + 2, NCHUNK, send_y, 0)

    BS, BR, GS = r["BS"], r["BR"], r["GS"]

    def scale_part(j, carry):
        lanes = pl.ds(aligned(j * CW, CW), CW)
        rows = pl.ds(aligned(j * CW, CW), CW)
        pair = dot(CF[:, lanes], ACT[...], 0, 0)
        weight = W[1, rows, :].astype(F32)
        GS[j] = lane_sums(pair * weight)
        return carry

    lax.fori_loop(0, NCHAN, scale_part, 0)

    if first:
        images_third(1)

    def far_wait(s, carry):
        far_copy(s).wait_recv()
        return carry

    lax.fori_loop(0, SLOTS, far_wait, 0)
    dnormed = DN[...] + R2[...].astype(F32)
    DN[...] = dnormed
    xhat = X[...]
    dxhat = dnormed * chan_row(TAPS + 1)
    sums = two_rows(lane_sums(dxhat), lane_sums(dxhat * xhat))
    for j in range(NCHAN):
        BS[j, :, 0:ROWS] = sums
        BS[j, :, ROWS:STATW] = GS[j]
    BR[chan] = BS[chan]
    back = [
        push(BS.at[c], BR.at[chan], d)
        for c, d in ((c_core, d_core), (c_side, d_side), (c_diag, d_diag))
    ]

    def mats_part(j, carry):
        lanes = pl.ds(aligned(j * CW, CW), CW)
        F2[0, lanes, :] = dot(NF[:, lanes], DH[...], 0, 0)
        F2[1, lanes, :] = dot(DB[:, lanes], ACT[...], 0, 0)
        return carry

    lax.fori_loop(0, NCHAN, mats_part, 0)
    if first:
        f_out = local(F2, r["fm"].at[0])

    for copy in back:
        copy.wait_recv()
    totals = BR[0] + BR[1] + BR[2] + BR[3]
    mean_a, mean_b = two_columns(
        totals[0:1, 0:ROWS] * (1.0 / C), totals[1:2, 0:ROWS] * (1.0 / C)
    )
    dnormed = DN[...]
    xhat = X[...]
    dconv = (dnormed * chan_row(TAPS + 1) - mean_a - xhat * mean_b) * r["INV"][...]
    DC, FC = r["DC"], r["FC"]
    DC[...] = dconv.reshape(SLOTS, SIDE, PADW, CW)
    FC[TAPS] = jnp.sum(dconv, 0, keepdims=True)
    FC[TAPS + 1] = jnp.sum(dnormed * xhat, 0, keepdims=True)
    FC[TAPS + 2] = jnp.sum(dnormed, 0, keepdims=True)
    FC[TAPS + 3] = chan_row(TAPS + 4) * inv * cot_sum
    FC[TAPS + 4] = inv * (totals[0:1, ROWS:STATW] + chan_row(TAPS + 3) * cot_sum)

    def tap_column(v, carry):
        def over(s, accs):
            grad = DC[s]
            return tuple(
                accs[u] + jnp.sum(SH[v, s, u : u + SIDE] * grad, 0) for u in range(KS)
            )

        accs = lax.fori_loop(0, SLOTS, over, tuple(jnp.zeros((PADW, CW), F32) for _ in range(KS)))
        for u in range(KS):
            FC[u * KS + v] = jnp.sum(accs[u], 0, keepdims=True)
        return carry

    lax.fori_loop(0, KS, tap_column, 0)

    fresh = FC[...]
    r["new_yc"][...] = 0.5 * (r["yc"][...] + r["RYC"][...]) + fresh - r["gc"][...]
    r["new_yb"][...] = 0.5 * (r["yb"][...] + r["RYB"][...]) + GB[...] - r["gb"][...]
    if first:
        r["fc"][...] = fresh
        r["fb"][...] = GB[...]
        images_end(1)
        for s in range(SLOTS):
            for h in range(2):
                r["picked_next"][s, h * HALF : (h + 1) * HALF] = picked(1, h, s)

    g_in.wait()
    out_sem = take("local", NCHUNK)

    def y_out(i):
        return pltpu.make_async_copy(
            piece(Y2, i), piece(r["new_ym"].at[0], i), r["local"].at[out_sem + i]
        )

    def track(i, carry):
        y_copy(i).wait_recv()
        at_i = rows_of(i)
        Y2[at_i] = 0.5 * (Y2[at_i] + YP[at_i].astype(F32)) + F2[at_i] - G2[at_i]
        y_out(i).start()
        return carry

    lax.fori_loop(0, NCHUNK, track, 0)

    def swaps_end(i, carry):
        p_copy(i).wait_send()
        y_copy(i).wait_send()
        y_out(i).wait()
        return carry

    lax.fori_loop(0, NCHUNK, swaps_end, 0)

    def slots_end(s, carry):
        norm_core(s).wait_send()
        norm_side(s).wait_send()
        norm_far(s).wait_send()
        near_copy(s, 0).wait_send()
        near_copy(s, 1).wait_send()
        far_copy(s).wait_send()
        return carry

    lax.fori_loop(0, SLOTS, slots_end, 0)
    for wait in ends:
        wait()
    q_out.wait()
    if first:
        f_out.wait()


def iteration(t, hop, state, images, cot, ids, counts):
    first = t == 0
    pm, pc, pb, ym, yc, yb, gm, gc, gb = state
    hbm = pl.BlockSpec(memory_space=pl.ANY)
    vmem = pl.BlockSpec(memory_space=pltpu.VMEM)
    smem = pl.BlockSpec(memory_space=pltpu.SMEM)
    ins = [("images", images, hbm), ("ids", ids, smem)] if first else [("picked", images, vmem)]
    ins += [("counts", counts, smem), ("cot", cot, hbm)]
    ins += [("pm", pm, hbm), ("pc", pc, vmem), ("pb", pb, vmem)]
    ins += [("ym", ym, hbm), ("yc", yc, vmem), ("yb", yb, vmem)]
    ins += [("gm", gm, hbm), ("gc", gc, vmem), ("gb", gb, vmem)]
    outs = [("qm", pm, hbm), ("qc", pc, vmem), ("qb", pb, vmem)]
    outs += [("new_ym", ym, hbm), ("new_yc", yc, vmem), ("new_yb", yb, vmem)]
    if first:
        outs += [("fm", gm, hbm), ("fc", gc, vmem), ("fb", gb, vmem)]
        outs += [("picked_next", jax.ShapeDtypeStruct((SLOTS, SIDE, PADW, CW), BF16), vmem)]
    V = pltpu.VMEM
    mats = (2, C, HID)
    half = (HALF, PADW, CW)
    scratch = {n: V(mats, F32) for n in ("P2", "Y2", "G2", "F2")}
    scratch |= {n: V(mats, BF16) for n in ("PB", "PP", "YB", "YP", "W")}
    scratch |= {n: V((ROWS, C), BF16) for n in ("NF", "CF", "DB", "ACT", "DH")}
    scratch |= {n: V((ROWS, CW), F32) for n in ("X", "INV", "DN")}
    scratch |= {n: V((ROWS, CW), BF16) for n in ("S2", "R2")}
    scratch |= {n: V((SLOTS, SIDE, PADW, CW), F32) for n in ("DC",)}
    scratch |= {n: V((NCHAN, 8, STATW), F32) for n in ("STR", "BS", "BR")}
    scratch |= {n: V((TAPS + 5, 1, CW), F32) for n in ("RPC", "RYC", "FC")}
    scratch |= {n: V((1, HID), F32) for n in ("RPB", "RYB", "GB")}
    scratch |= {
        "DP": V((ROWS, C), F32),
        "R1": V((2, ROWS, CW), F32),
        "GS": V((NCHAN, 8, CW), F32),
        "XP": V((SLOTS, SIDE + 6, 24, CW), F32),
        "SH": V((KS, SLOTS, SIDE + 6, PADW, CW), F32),
        "send": pltpu.SemaphoreType.DMA((128,)),
        "recv": pltpu.SemaphoreType.DMA((128,)),
        "local": pltpu.SemaphoreType.DMA((32,)),
    }
    if first:
        for u in range(2):
            for h in range(2):
                scratch["G%d%d" % (u, h)] = V((16,) + half, BF16)
                scratch["XR%d%d" % (u, h)] = V((4, SLOTS) + half, BF16)
        scratch |= {
            "XS": V((2, 2, 3, SLOTS) + half, BF16),
            "IDV": V((2, 4, 8, 128), jnp.int32),
            "IDS": pltpu.SMEM((2, 4, 8, 128), jnp.int32),
        }
    names = [n for n, _, _ in ins] + [n for n, _, _ in outs] + list(scratch)
    return pl.pallas_call(
        functools.partial(kernel, t, hop, names),
        out_shape=[jax.ShapeDtypeStruct(a.shape, a.dtype) for _, a, _ in outs],
        in_specs=[s for _, _, s in ins],
        out_specs=[s for _, _, s in outs],
        scratch_shapes=list(scratch.values()),
        compiler_params=pltpu.CompilerParams(
            collective_id=t * 3 + hop,
            has_side_effects=True,
            vmem_limit_bytes=58 * 1024 * 1024,
        ),
    )(*[a for _, a, _ in ins])


def copies(n, *refs):
    arrays, results, held, (sem_in, sem_out) = refs[:n], refs[n : 2 * n], refs[2 * n : 3 * n], refs[3 * n :]

    def pieces(k):
        return [(0, i) for i in range(2)] if k % 3 == 0 else [()]

    def pick(ref, index):
        return ref.at[index] if index else ref

    moves = []
    for k in range(n):
        for index in pieces(k):
            moves.append((k, index, len(moves)))
    into = [
        pltpu.make_async_copy(pick(arrays[k], i), pick(held[k], i), sem_in.at[m])
        for k, i, m in moves
    ]
    out = [
        pltpu.make_async_copy(pick(held[k], i), pick(results[k], i), sem_out.at[m])
        for k, i, m in moves
    ]
    for copy in into:
        copy.start()
    for first, second in zip(into, out):
        first.wait()
        second.start()
    for copy in out:
        copy.wait()


def handed_on(values):
    n = len(values)
    hbm = pl.BlockSpec(memory_space=pl.ANY)
    return pl.pallas_call(
        functools.partial(copies, n),
        out_shape=[jax.ShapeDtypeStruct(a.shape, a.dtype) for a in values],
        in_specs=[hbm] * n,
        out_specs=[hbm] * n,
        scratch_shapes=[pltpu.VMEM(a.shape, a.dtype) for a in values]
        + [pltpu.SemaphoreType.DMA((n + 2,))] * 2,
        compiler_params=pltpu.CompilerParams(vmem_limit_bytes=16 * 1024 * 1024),
    )(*values)


def on_device(images, cotangent, image_ids, counts, hop_exponents, *state):
    def padded(maps):
        return jnp.pad(maps, ((0, 0), (0, 0), (0, 0), (0, PADW - SIDE), (0, 0)))

    images = padded(images)
    cot = padded(cotangent[:, 0]).reshape(ITERS, ROWS, CW)
    counts = counts.T

    def turned(values):
        return tuple(a.transpose(1, 0, 2) if i % 3 == 1 else a for i, a in enumerate(values))

    def branch(t, hop):
        def run(operands):
            source, state = operands
            return iteration(t, hop, state, source, cot, image_ids, counts)

        return run

    def step(t, source, state):
        return lax.switch(
            hop_exponents[t], [branch(t, hop) for hop in range(3)], (source, state)
        )

    out = step(0, images, turned(state))
    return turned(handed_on(step(1, out[9], tuple(out[:9]))))


def solution(mesh):
    mats, chans, bias = P("peer", None, None, "chan"), P("peer", None, "chan"), P("peer", "chan")
    in_specs = (
        P(None, "peer", None, None, "chan"),
        P(None, "peer", None, None, None, "chan"),
        P(None, "peer", None),
        P(None, "peer"),
        P(),
    ) + (mats, chans, bias) * 3
    return jax.shard_map(
        on_device, mesh=mesh, in_specs=in_specs, out_specs=(mats, chans, bias) * 2, check_vma=False
    )
```

```python
import functools

import jax
import jax.numpy as jnp
from jax import lax
from jax.experimental import pallas as pl
from jax.experimental.pallas import tpu as pltpu
from jax.sharding import PartitionSpec as P

KS = 7
TAPS = KS * KS
ITERS = 2
EPS = 1e-06
LEARNING_RATE = 0.01
MESH = pl.DeviceIdType.MESH
F32 = jnp.float32
BF16 = jnp.bfloat16

SIDE = 14
PADW = 16
HALF = SIDE // 2
SLOTS = 4
SROWS = SIDE * PADW
ROWS = SLOTS * SROWS
CW = 128
C = 512
HID = 512
NCHUNK = 8
CROWS = 128
NCHAN = 4
STATW = ROWS + CW


def aligned(value, step):
    return pl.multiple_of(value, step)


def dot(a, b, ca, cb):
    return lax.dot_general(a, b, (((ca,), (cb,)), ((), ())), preferred_element_type=F32)


def terms_of(values, terms):
    parts = []
    for _ in range(terms):
        part = values.astype(BF16)
        parts.append(part)
        values = values - part.astype(F32)
    return parts


def lane_sums(values, terms=2):
    ones = jnp.ones((8, values.shape[1]), BF16)
    total = None
    for part in terms_of(values, terms):
        here = dot(ones, part, 1, 1)
        total = here if total is None else total + here
    return total


def two_rows(first, second):
    row = lax.broadcasted_iota(jnp.int32, (8, first.shape[-1]), 0)
    return jnp.where(row == 0, first, jnp.where(row == 1, second, 0.0))


def two_columns(first, second):
    row = lax.broadcasted_iota(jnp.int32, (16, first.shape[-1]), 0)
    rows = jnp.zeros((16, first.shape[-1]), F32)
    for k, part in enumerate(terms_of(first, 3) + terms_of(second, 3)):
        rows = jnp.where(row == k, part.astype(F32), rows)
    row = lax.broadcasted_iota(jnp.int32, (16, 2 * CW), 0)
    lane = lax.broadcasted_iota(jnp.int32, (16, 2 * CW), 1)
    offset = row - jnp.where(lane < CW, 0, 3)
    pick = jnp.where((offset >= 0) & (offset < 3), 1.0, 0.0)
    both = dot(rows.astype(BF16), pick.astype(BF16), 0, 0)
    return both[:, :CW], both[:, CW:]


def kernel(t, hop, names, *refs):
    r = dict(zip(names, refs))
    first = t == 0
    peer = lax.axis_index("peer")
    chan = lax.axis_index("chan")
    my_z, my_y, my_x = peer % 4, (peer // 4) % 2, peer // 8
    core, side = chan % 2, chan // 2

    def at(new_peer, new_chan):
        return (new_peer, new_chan)

    c_core = side * 2 + 1 - core
    c_side = (1 - side) * 2 + core
    c_diag = (1 - side) * 2 + 1 - core
    d_core, d_side, d_diag = at(peer, c_core), at(peer, c_side), at(peer, c_diag)
    bit = (peer // (2**hop)) % 2
    d_hop = at(peer + (1 - 2 * bit) * (2**hop), chan)
    mine = {"x": my_x, "y": my_y, "z": my_z}
    count_of = {"x": 4, "y": 2, "z": 4}
    stride_of = {"x": 8, "y": 4, "z": 1}
    to, source, line = {}, {}, {}
    for dim, n in count_of.items():
        to[dim] = [(mine[dim] + d) % n for d in range(1, n)]
        source[dim] = [(mine[dim] + n - d) % n for d in range(1, n)]
        line[dim] = [at(peer + (c - mine[dim]) * stride_of[dim], chan) for c in to[dim]]

    counters = {"remote": 0, "local": 0}
    ends = []

    def take(kind, n):
        start = counters[kind]
        counters[kind] += n
        return start

    def remote(src, dst, device, index):
        return pltpu.make_async_remote_copy(
            src_ref=src,
            dst_ref=dst,
            send_sem=r["send"].at[index],
            recv_sem=r["recv"].at[index],
            device_id=device,
            device_id_type=MESH,
        )

    def push(src, dst, device):
        copy = remote(src, dst, device, take("remote", 1))
        copy.start()
        ends.append(copy.wait_send)
        return copy

    def local(src, dst):
        copy = pltpu.make_async_copy(src, dst, r["local"].at[take("local", 1)])
        copy.start()
        return copy

    P2, Y2, G2, F2 = r["P2"], r["Y2"], r["G2"], r["F2"]
    PB, PP, YB, YP, W = r["PB"], r["PP"], r["YB"], r["YP"], r["W"]

    def piece(ref, i):
        return ref.at[i // 4, pl.ds(aligned((i % 4) * CROWS, CROWS), CROWS), :]

    if first:
        G = [[r["G%d%d" % (u, h)] for h in range(2)] for u in range(2)]
        plan = ("yzx", "yxz") if hop == 2 else ("zyx", "zyx")
        order = {(u, h): plan[h] for u in range(2) for h in range(2)}

        def block(u, h, near, far):
            return G[u][h].at[pl.ds((near * count_of[order[u, h][1]] + far) * 2, 2)]

        def own_block(u, h):
            return block(u, h, mine[order[u, h][0]], mine[order[u, h][1]])

        img_in = {
            (u, h): local(r["images"].at[u, :, pl.ds(h * HALF, HALF)], own_block(u, h))
            for u in range(2)
            for h in range(2)
        }
    p_sem = take("local", NCHUNK)

    def p_load(i):
        return pltpu.make_async_copy(
            piece(r["pm"].at[0], i), piece(P2, i), r["local"].at[p_sem + i]
        )

    def start_p(i, carry):
        p_load(i).start()
        return carry

    lax.fori_loop(0, NCHUNK, start_p, 0)
    CF = r["CF"]
    my_lanes = pl.ds(aligned(chan * CW, CW), CW)
    side_lanes = pl.ds(aligned(c_side * CW, CW), CW)
    cot_in = local(r["cot"].at[t], CF.at[:, my_lanes])
    y_in = local(r["ym"].at[0], Y2)
    g_in = local(r["gm"].at[0], G2)

    count = r["counts"][0, t]

    def valid(s):
        return jnp.where(s < count, 1.0, 0.0).astype(F32)

    inv = 1.0 / jnp.full((1, CW), count.astype(F32))

    if first:
        IDV = r["IDV"]
        lane = lax.broadcasted_iota(jnp.int32, (8, 128), 1)
        row = lax.broadcasted_iota(jnp.int32, (8, 128), 0)
        tile = jnp.zeros((8, 128), jnp.int32)
        for u in range(2):
            for s in range(SLOTS):
                tile = jnp.where((row == u) & (lane == s), r["ids"][u, 0, s], tile)
        IDV[0, my_x] = tile
        IDV[1, my_z] = tile

    barrier = pltpu.get_barrier_semaphore()
    greet = [d_core, d_side, d_diag] + (line["y"] + line["z"] + line["x"] if first else [d_hop])
    for device in greet:
        pl.semaphore_signal(barrier, inc=1, device_id=device, device_id_type=MESH)
    pl.semaphore_wait(barrier, len(greet))

    small = [
        push(r["pc"], r["RPC"], d_hop),
        push(r["pb"], r["RPB"], d_hop),
        push(r["yc"], r["RYC"], d_hop),
        push(r["yb"], r["RYB"], d_hop),
    ]

    fetch = {}
    if first:
        fetch["ids"] = [
            push(IDV.at[k, mine[dim]], IDV.at[k, mine[dim]], d)
            for k, dim in enumerate("xz")
            for d in line[dim]
        ]

    def images_begin(u):
        for h in range(2):
            near, far, _ = order[u, h]
            img_in[u, h].wait()
            own = own_block(u, h)
            fetch["near", u, h] = [push(own, own, d) for d in line[near]]
            fetch["far", u, h] = [push(own, own, d) for d in line[far]]

    def images_second(u):
        for h in range(2):
            near, far, _ = order[u, h]
            for copy, place in zip(fetch["near", u, h], source[near]):
                copy.wait_recv()
                part = block(u, h, place, mine[far])
                fetch["far", u, h] += [push(part, part, d) for d in line[far]]

    def place_of(ident, dim):
        return (ident // (2 * stride_of[dim])) % count_of[dim]

    def images_third(u):
        for h in range(2):
            near, far, last = order[u, h]
            for copy in fetch["far", u, h]:
                copy.wait_recv()
            XS, XR = r["XS"], r["XR%d%d" % (u, h)]

            def wanted(c, s):
                ident = r["IDS"]["xz".index(last), c, u, s]
                row = place_of(ident, near) * count_of[far] + place_of(ident, far)
                return G[u][h][row * 2 + ident % 2]

            fetch["x", u, h] = []
            for j in range(3):
                for s in range(SLOTS):
                    XS[u, h, j, s] = wanted(to[last][j], s)
                fetch["x", u, h].append(push(XS.at[u, h, j], XR.at[mine[last]], line[last][j]))
            for s in range(SLOTS):
                XR[mine[last], s] = wanted(mine[last], s)

    def images_end(u):
        for h in range(2):
            for copy in fetch["x", u, h]:
                copy.wait_recv()

    def picked(u, h, s):
        return r["XR%d%d" % (u, h)][place_of(r["ids"][u, 0, s], order[u, h][2]), s]

    if first:
        images_begin(0)

    p_send = take("remote", NCHUNK)

    def p_copy(i):
        return remote(piece(PB, i), piece(PP, i), d_hop, p_send + i)

    def rows_of(i):
        return (i // 4, pl.ds(aligned((i % 4) * CROWS, CROWS), CROWS), slice(None))

    def send_p(i, carry):
        p_load(i).wait()
        PB[rows_of(i)] = P2[rows_of(i)].astype(BF16)
        p_copy(i).start()
        return carry

    lax.fori_loop(0, NCHUNK, send_p, 0)

    r["XP"][...] = jnp.zeros_like(r["XP"])
    cot_in.wait()
    cot_sum = jnp.zeros((1, CW), F32)
    for s in range(SLOTS):
        rows = slice(s * SROWS, (s + 1) * SROWS)
        live = CF[rows, my_lanes].astype(F32) * valid(s)
        CF[rows, my_lanes] = live.astype(BF16)
        cot_sum = cot_sum + jnp.sum(live, 0, keepdims=True)
    cot_core = push(CF.at[:, my_lanes], CF.at[:, my_lanes], d_core)
    cot_side = push(CF.at[:, my_lanes], CF.at[:, my_lanes], d_side)

    XP, SH, X = r["XP"], r["SH"], r["X"]

    def windows():
        for s in range(SLOTS):
            for h in range(2):
                image = picked(0, h, s) if first else r["picked"][s, h * HALF : (h + 1) * HALF]
                top = 3 + h * HALF
                XP[s, top : top + HALF, 3 : 3 + PADW, :] = image.astype(F32) * valid(s)

        def shift(s, carry):
            for v in range(KS):
                SH[v, s] = XP[s, :, v : v + PADW, :]
            return carry

        lax.fori_loop(0, SLOTS, shift, 0)

    if not first:
        windows()

    for copy in small:
        copy.wait_recv()
    qc, qb = r["qc"], r["qb"]
    qc[...] = 0.5 * (r["pc"][...] + r["RPC"][...]) - LEARNING_RATE * r["yc"][...]
    qb[...] = 0.5 * (r["pb"][...] + r["RPB"][...]) - LEARNING_RATE * r["yb"][...]

    def chan_row(k):
        return qc[k]

    if first:
        images_second(0)
        for copy in fetch["ids"]:
            copy.wait_recv()
        ids_in = local(IDV, r["IDS"])
        ids_in.wait()
        images_third(0)
        images_end(0)
        images_begin(1)

    if first:
        windows()

    def conv_slot(s, carry):
        def column(v, acc):
            for u in range(KS):
                acc = acc + SH[v, s, u : u + SIDE] * qc[u * KS + v]
            return acc

        acc = lax.fori_loop(0, KS, column, jnp.zeros((SIDE, PADW, CW), F32))
        X[pl.ds(aligned(s * SROWS, SROWS), SROWS), :] = acc.reshape(SROWS, CW) + chan_row(TAPS)
        return carry

    lax.fori_loop(0, SLOTS, conv_slot, 0)

    STR = r["STR"]
    conv_out = X[...]
    mean_here = jnp.sum(conv_out, 1, keepdims=True) * (1.0 / CW)
    centred = conv_out - mean_here
    mean_row = lane_sums(conv_out, 3) * (1.0 / CW)
    STR[chan, :, 0:ROWS] = two_rows(mean_row, lane_sums(centred * centred))
    STR[chan, :, ROWS:STATW] = jnp.broadcast_to(chan_row(TAPS + 4), (8, CW))
    stats = [push(STR.at[chan], STR.at[chan], d) for d in (d_core, d_side, d_diag)]
    cot_side.wait_recv()
    cot_far = push(CF.at[:, side_lanes], CF.at[:, side_lanes], d_core)
    for copy in stats:
        copy.wait_recv()
    means = [STR[j, 0:1, 0:ROWS] for j in range(NCHAN)]
    mean = (means[0] + means[1] + means[2] + means[3]) * 0.25
    squares = STR[0, 1:2, 0:ROWS] + STR[1, 1:2, 0:ROWS] + STR[2, 1:2, 0:ROWS] + STR[3, 1:2, 0:ROWS]
    for j in range(NCHAN):
        squares = squares + CW * (means[j] - mean) * (means[j] - mean)
    deviation = lax.rsqrt(squares * (1.0 / C) + EPS)
    mean_col, inv_col = two_columns(mean, deviation)
    r["INV"][...] = inv_col
    xhat = (X[...] - mean_col) * inv_col
    X[...] = xhat
    NF = r["NF"]
    NF[:, my_lanes] = (xhat * chan_row(TAPS + 1) + chan_row(TAPS + 2)).astype(BF16)

    na, nb, nc = take("remote", SLOTS), take("remote", SLOTS), take("remote", SLOTS)

    def slot_rows(s):
        return pl.ds(aligned(s * SROWS, SROWS), SROWS)

    def norm_core(s):
        part = NF.at[slot_rows(s), my_lanes]
        return remote(part, part, d_core, na + s)

    def norm_side(s):
        part = NF.at[slot_rows(s), my_lanes]
        return remote(part, part, d_side, nb + s)

    def norm_far(s):
        part = NF.at[slot_rows(s), side_lanes]
        return remote(part, part, d_core, nc + s)

    def norm_send(s, carry):
        norm_side(s).start()
        norm_core(s).start()
        return carry

    lax.fori_loop(0, SLOTS, norm_send, 0)

    if first:
        images_second(1)

    cot_core.wait_recv()
    cot_far.wait_recv()
    DB = r["DB"]
    for j in range(NCHAN):
        lanes = slice(j * CW, (j + 1) * CW)
        factor = inv * STR[j, 0:1, ROWS:STATW]
        DB[:, lanes] = (CF[:, lanes].astype(F32) * factor).astype(BF16)

    y_in.wait()

    def mix(i, carry):
        p_copy(i).wait_recv()
        q = 0.5 * (P2[rows_of(i)] + PP[rows_of(i)].astype(F32)) - LEARNING_RATE * Y2[rows_of(i)]
        P2[rows_of(i)] = q
        W[rows_of(i)] = q.astype(BF16)
        return carry

    lax.fori_loop(0, NCHUNK, mix, 0)
    q_out = local(P2, r["qm"].at[0])

    y_send = take("remote", NCHUNK)

    def y_copy(i):
        return remote(piece(YB, i), piece(YP, i), d_hop, y_send + i)

    def send_y(i, carry):
        YB[rows_of(i)] = Y2[rows_of(i)].astype(BF16)
        y_copy(i).start()
        return carry

    if hop != 2:
        lax.fori_loop(0, NCHUNK, send_y, 0)

    ACT, DH, DP, R1, S2, R2, DN = (r[n] for n in ("ACT", "DH", "DP", "R1", "S2", "R2", "DN"))
    r1, r2 = take("remote", 2 * SLOTS), take("remote", SLOTS)

    def near_copy(s, b):
        lanes = pl.ds(aligned((b * 2 + 1 - core) * CW, CW), CW)
        return remote(DP.at[slot_rows(s), lanes], R1.at[b, slot_rows(s)], d_core, r1 + 2 * s + b)

    def far_copy(s):
        return remote(S2.at[slot_rows(s)], R2.at[slot_rows(s)], d_side, r2 + s)

    GB = r["GB"]
    GB[...] = jnp.zeros_like(GB)

    def slot_step(step, carry):
        if hop == 2:
            send_y(step, carry)

        @pl.when(step < SLOTS)
        def _():
            norm_side(step).wait_recv()
            norm_far(step).start()

        @pl.when((step > 0) & (step <= SLOTS))
        def _():
            s = step - 1
            norm_core(s).wait_recv()
            norm_far(s).wait_recv()
            rows = slot_rows(s)
            hidden = dot(NF[rows, :], W[0], 1, 0) + qb[...]
            cdf = 0.5 * (1.0 + lax.erf(hidden * 0.7071067811865476))
            density = jnp.exp(-0.5 * hidden * hidden) * 0.3989422804014327
            ACT[rows, :] = (hidden * cdf).astype(BF16)
            slope = cdf + hidden * density
            dhidden = dot(DB[rows, :], W[1], 1, 0) * slope
            GB[...] += jnp.sum(dhidden, 0, keepdims=True)
            low = dhidden.astype(BF16)
            DH[rows, :] = low
            DP[rows, :] = dot(low, W[0], 1, 1)
            near_copy(s, 0).start()
            near_copy(s, 1).start()

        @pl.when(step > 1)
        def _():
            s = step - 2
            rows = slot_rows(s)
            near_copy(s, 0).wait_recv()
            near_copy(s, 1).wait_recv()
            S2[rows, :] = (DP[rows, side_lanes] + R1[1 - side, rows, :]).astype(BF16)
            far_copy(s).start()
            DN[rows, :] = DP[rows, my_lanes] + R1[side, rows, :]

        return carry

    lax.fori_loop(0, SLOTS + 2, slot_step, 0)
    if hop == 2:
        lax.fori_loop(SLOTS + 2, NCHUNK, send_y, 0)

    BS, BR, GS = r["BS"], r["BR"], r["GS"]

    def scale_part(j, carry):
        lanes = pl.ds(aligned(j * CW, CW), CW)
        rows = pl.ds(aligned(j * CW, CW), CW)
        pair = dot(CF[:, lanes], ACT[...], 0, 0)
        weight = W[1, rows, :].astype(F32)
        GS[j] = lane_sums(pair * weight)
        return carry

    lax.fori_loop(0, NCHAN, scale_part, 0)

    if first:
        images_third(1)

    def far_wait(s, carry):
        far_copy(s).wait_recv()
        return carry

    lax.fori_loop(0, SLOTS, far_wait, 0)
    dnormed = DN[...] + R2[...].astype(F32)
    DN[...] = dnormed
    xhat = X[...]
    dxhat = dnormed * chan_row(TAPS + 1)
    sums = two_rows(lane_sums(dxhat), lane_sums(dxhat * xhat))
    for j in range(NCHAN):
        BS[j, :, 0:ROWS] = sums
        BS[j, :, ROWS:STATW] = GS[j]
    BR[chan] = BS[chan]
    back = [
        push(BS.at[c], BR.at[chan], d)
        for c, d in ((c_core, d_core), (c_side, d_side), (c_diag, d_diag))
    ]

    def mats_part(j, carry):
        lanes = pl.ds(aligned(j * CW, CW), CW)
        F2[0, lanes, :] = dot(NF[:, lanes], DH[...], 0, 0)
        F2[1, lanes, :] = dot(DB[:, lanes], ACT[...], 0, 0)
        return carry

    lax.fori_loop(0, NCHAN, mats_part, 0)
    if first:
        f_out = local(F2, r["fm"].at[0])

    for copy in back:
        copy.wait_recv()
    totals = BR[0] + BR[1] + BR[2] + BR[3]
    mean_a, mean_b = two_columns(
        totals[0:1, 0:ROWS] * (1.0 / C), totals[1:2, 0:ROWS] * (1.0 / C)
    )
    dnormed = DN[...]
    xhat = X[...]
    dconv = (dnormed * chan_row(TAPS + 1) - mean_a - xhat * mean_b) * r["INV"][...]
    DC, FC = r["DC"], r["FC"]
    DC[...] = dconv.reshape(SLOTS, SIDE, PADW, CW)
    FC[TAPS] = jnp.sum(dconv, 0, keepdims=True)
    FC[TAPS + 1] = jnp.sum(dnormed * xhat, 0, keepdims=True)
    FC[TAPS + 2] = jnp.sum(dnormed, 0, keepdims=True)
    FC[TAPS + 3] = chan_row(TAPS + 4) * inv * cot_sum
    FC[TAPS + 4] = inv * (totals[0:1, ROWS:STATW] + chan_row(TAPS + 3) * cot_sum)

    def tap_column(v, carry):
        def over(s, accs):
            grad = DC[s]
            return tuple(
                accs[u] + jnp.sum(SH[v, s, u : u + SIDE] * grad, 0) for u in range(KS)
            )

        accs = lax.fori_loop(0, SLOTS, over, tuple(jnp.zeros((PADW, CW), F32) for _ in range(KS)))
        for u in range(KS):
            FC[u * KS + v] = jnp.sum(accs[u], 0, keepdims=True)
        return carry

    lax.fori_loop(0, KS, tap_column, 0)

    fresh = FC[...]
    r["new_yc"][...] = 0.5 * (r["yc"][...] + r["RYC"][...]) + fresh - r["gc"][...]
    r["new_yb"][...] = 0.5 * (r["yb"][...] + r["RYB"][...]) + GB[...] - r["gb"][...]
    if first:
        r["fc"][...] = fresh
        r["fb"][...] = GB[...]
        images_end(1)
        for s in range(SLOTS):
            for h in range(2):
                r["picked_next"][s, h * HALF : (h + 1) * HALF] = picked(1, h, s)

    g_in.wait()
    out_sem = take("local", NCHUNK)

    def y_out(i):
        return pltpu.make_async_copy(
            piece(Y2, i), piece(r["new_ym"].at[0], i), r["local"].at[out_sem + i]
        )

    def track(i, carry):
        y_copy(i).wait_recv()
        at_i = rows_of(i)
        Y2[at_i] = 0.5 * (Y2[at_i] + YP[at_i].astype(F32)) + F2[at_i] - G2[at_i]
        y_out(i).start()
        return carry

    lax.fori_loop(0, NCHUNK, track, 0)

    def swaps_end(i, carry):
        p_copy(i).wait_send()
        y_copy(i).wait_send()
        y_out(i).wait()
        return carry

    lax.fori_loop(0, NCHUNK, swaps_end, 0)

    def slots_end(s, carry):
        norm_core(s).wait_send()
        norm_side(s).wait_send()
        norm_far(s).wait_send()
        near_copy(s, 0).wait_send()
        near_copy(s, 1).wait_send()
        far_copy(s).wait_send()
        return carry

    lax.fori_loop(0, SLOTS, slots_end, 0)
    for wait in ends:
        wait()
    q_out.wait()
    if first:
        f_out.wait()


def iteration(t, hop, state, images, cot, ids, counts):
    first = t == 0
    pm, pc, pb, ym, yc, yb, gm, gc, gb = state
    hbm = pl.BlockSpec(memory_space=pl.ANY)
    vmem = pl.BlockSpec(memory_space=pltpu.VMEM)
    smem = pl.BlockSpec(memory_space=pltpu.SMEM)
    ins = [("images", images, hbm), ("ids", ids, smem)] if first else [("picked", images, vmem)]
    ins += [("counts", counts, smem), ("cot", cot, hbm)]
    ins += [("pm", pm, hbm), ("pc", pc, vmem), ("pb", pb, vmem)]
    ins += [("ym", ym, hbm), ("yc", yc, vmem), ("yb", yb, vmem)]
    ins += [("gm", gm, hbm), ("gc", gc, vmem), ("gb", gb, vmem)]
    outs = [("qm", pm, hbm), ("qc", pc, vmem), ("qb", pb, vmem)]
    outs += [("new_ym", ym, hbm), ("new_yc", yc, vmem), ("new_yb", yb, vmem)]
    if first:
        outs += [("fm", gm, hbm), ("fc", gc, vmem), ("fb", gb, vmem)]
        outs += [("picked_next", jax.ShapeDtypeStruct((SLOTS, SIDE, PADW, CW), BF16), vmem)]
    V = pltpu.VMEM
    mats = (2, C, HID)
    half = (HALF, PADW, CW)
    scratch = {n: V(mats, F32) for n in ("P2", "Y2", "G2", "F2")}
    scratch |= {n: V(mats, BF16) for n in ("PB", "PP", "YB", "YP", "W")}
    scratch |= {n: V((ROWS, C), BF16) for n in ("NF", "CF", "DB", "ACT", "DH")}
    scratch |= {n: V((ROWS, CW), F32) for n in ("X", "INV", "DN")}
    scratch |= {n: V((ROWS, CW), BF16) for n in ("S2", "R2")}
    scratch |= {n: V((SLOTS, SIDE, PADW, CW), F32) for n in ("DC",)}
    scratch |= {n: V((NCHAN, 8, STATW), F32) for n in ("STR", "BS", "BR")}
    scratch |= {n: V((TAPS + 5, 1, CW), F32) for n in ("RPC", "RYC", "FC")}
    scratch |= {n: V((1, HID), F32) for n in ("RPB", "RYB", "GB")}
    scratch |= {
        "DP": V((ROWS, C), F32),
        "R1": V((2, ROWS, CW), F32),
        "GS": V((NCHAN, 8, CW), F32),
        "XP": V((SLOTS, SIDE + 6, 24, CW), F32),
        "SH": V((KS, SLOTS, SIDE + 6, PADW, CW), F32),
        "send": pltpu.SemaphoreType.DMA((128,)),
        "recv": pltpu.SemaphoreType.DMA((128,)),
        "local": pltpu.SemaphoreType.DMA((32,)),
    }
    if first:
        for u in range(2):
            for h in range(2):
                scratch["G%d%d" % (u, h)] = V((16,) + half, BF16)
                scratch["XR%d%d" % (u, h)] = V((4, SLOTS) + half, BF16)
        scratch |= {
            "XS": V((2, 2, 3, SLOTS) + half, BF16),
            "IDV": V((2, 4, 8, 128), jnp.int32),
            "IDS": pltpu.SMEM((2, 4, 8, 128), jnp.int32),
        }
    names = [n for n, _, _ in ins] + [n for n, _, _ in outs] + list(scratch)
    return pl.pallas_call(
        functools.partial(kernel, t, hop, names),
        out_shape=[jax.ShapeDtypeStruct(a.shape, a.dtype) for _, a, _ in outs],
        in_specs=[s for _, _, s in ins],
        out_specs=[s for _, _, s in outs],
        scratch_shapes=list(scratch.values()),
        compiler_params=pltpu.CompilerParams(
            collective_id=t * 3 + hop,
            has_side_effects=True,
            vmem_limit_bytes=58 * 1024 * 1024,
        ),
    )(*[a for _, a, _ in ins])


def copies(n, *refs):
    arrays, results, held, (sem_in, sem_out) = refs[:n], refs[n : 2 * n], refs[2 * n : 3 * n], refs[3 * n :]

    def pieces(k):
        return [(0, i) for i in range(2)] if k % 3 == 0 else [()]

    def pick(ref, index):
        return ref.at[index] if index else ref

    moves = []
    for k in range(n):
        for index in pieces(k):
            moves.append((k, index, len(moves)))
    into = [
        pltpu.make_async_copy(pick(arrays[k], i), pick(held[k], i), sem_in.at[m])
        for k, i, m in moves
    ]
    out = [
        pltpu.make_async_copy(pick(held[k], i), pick(results[k], i), sem_out.at[m])
        for k, i, m in moves
    ]
    for copy in into:
        copy.start()
    for first, second in zip(into, out):
        first.wait()
        second.start()
    for copy in out:
        copy.wait()


def handed_on(values):
    n = len(values)
    hbm = pl.BlockSpec(memory_space=pl.ANY)
    return pl.pallas_call(
        functools.partial(copies, n),
        out_shape=[jax.ShapeDtypeStruct(a.shape, a.dtype) for a in values],
        in_specs=[hbm] * n,
        out_specs=[hbm] * n,
        scratch_shapes=[pltpu.VMEM(a.shape, a.dtype) for a in values]
        + [pltpu.SemaphoreType.DMA((n + 2,))] * 2,
        compiler_params=pltpu.CompilerParams(vmem_limit_bytes=16 * 1024 * 1024),
    )(*values)


def on_device(images, cotangent, image_ids, counts, hop_exponents, *state):
    def padded(maps):
        return jnp.pad(maps, ((0, 0), (0, 0), (0, 0), (0, PADW - SIDE), (0, 0)))

    images = padded(images)
    cot = padded(cotangent[:, 0]).reshape(ITERS, ROWS, CW)
    counts = counts.T

    def turned(values):
        return tuple(a.transpose(1, 0, 2) if i % 3 == 1 else a for i, a in enumerate(values))

    def branch(t, hop):
        def run(operands):
            source, state = operands
            return iteration(t, hop, state, source, cot, image_ids, counts)

        return run

    def step(t, source, state):
        return lax.switch(
            hop_exponents[t], [branch(t, hop) for hop in range(3)], (source, state)
        )

    out = step(0, images, turned(state))
    return turned(handed_on(step(1, out[9], tuple(out[:9]))))


def solution(mesh):
    mats, chans, bias = P("peer", None, None, "chan"), P("peer", None, "chan"), P("peer", "chan")
    in_specs = (
        P(None, "peer", None, None, "chan"),
        P(None, "peer", None, None, None, "chan"),
        P(None, "peer", None),
        P(None, "peer"),
        P(),
    ) + (mats, chans, bias) * 3
    return jax.shard_map(
        on_device, mesh=mesh, in_specs=in_specs, out_specs=(mats, chans, bias) * 2, check_vma=False
    )
```
